32 devices in a mesh: dom: 8 (over z, y), sub: 4 (over x, core).
Axes of the slice: x: 2, y: 2, z: 4, core: 2. Of those that a mesh axis runs over, the one named last changes fastest.
Arguments:
- displacement: float32 [3, 128, 289], P(None, ('dom', 'sub')), may hold values from -6 to 6
- macro_modulus: float32 [8, 32768], P(None, ('dom', 'sub')), may hold values from 0.5 to 4
- damaged_count: int32 [32], P(('dom', 'sub')), may hold values from 1 to 64, 1024 in all
- damaged_points: int32 [32, 64], P(('dom', 'sub')), may hold values from 0 to 8191, as said below
- damage: bfloat16 [2048, 4096], P(('dom', 'sub')), may hold values from 0 to 0.59765625
- voxel_modulus: bfloat16 [2048, 4096], P(('dom', 'sub')), may hold values from 0.5 to 4
Outputs:
- nodal_force: float32 [3, 128, 289], P(None, ('dom', 'sub'))
- new_damage: bfloat16 [2048, 4096], P(('dom', 'sub'))
The draws below stay inside these ranges and needn't reach their ends.
Inputs may be any that keep to these rules, and one draw needn't show every extreme that they name: `damaged_count`: the counts of all partitions sum to 1024, and the largest is 64. `damaged_points`: each row names 64 different points of its partition; the first damaged_count of them are the damaged ones; partition 0 lists point 0 and point 8 * 4 * 16^2 - 1.
All inputs are finite; a program needn't handle non-finite values. No bound on the sum of `damaged_count` on one device may be relied on, other than what follows from the above.
Results may differ from the reference program's by a relative error of at most 0.0055.
Values may be sent and summed in bfloat16 or wider, within the bound.
A program may use at most 64 MiB of HBM per device.

```python
import math
import jax
import jax.numpy as jnp
import numpy as np
from jax import lax

CELL = 16
SWEEPS = 2
EXY = 16
LZ = 4
DMG_DEV = 64
DOMAINS = 32
NZ = 128
NODES = 289
ELEMS = 32768
SLOTS = 2048
DMG_SUM = 1024
VOX = 4096


def draw_damaged_points(key, part):
    point_total = 8 * LZ * EXY * EXY
    ceiling = 2 ** 30 // point_total
    scores = jax.random.randint(key, (DOMAINS, point_total), 0, ceiling) * point_total + jnp.arange(point_total)[None, :]
    scores = scores.at[0, 0].set(ceiling * point_total).at[0, point_total - 1].set(ceiling * point_total + 1)
    top_values, picked = lax.top_k(scores, DMG_DEV)
    return picked.astype(jnp.int32)


def block_levels(rng, extent, pieces, low, top_value):
    level, own = 1.0, jax.random.fold_in(rng, 6)
    for position, parts in pieces:
        steps = jnp.exp(jax.random.uniform(jax.random.fold_in(own, position), (parts,), jnp.float32, low / len(pieces), top_value / len(pieces)))
        level = level * jnp.repeat(steps, extent[position] // parts).reshape([-1 if axis == position else 1 for axis in range(len(extent))])
    return level


def split_up(number_of, total, reach, slope):
    portions = [(1 << 20) // math.isqrt(standing ** slope) + 1 for standing in range(2, number_of + 1)]
    rest, holding = total - reach - (number_of - 1), [1] * (number_of - 1)
    while rest > 0:
        free = [i for i in range(number_of - 1) if holding[i] < reach]
        pool, remaining = sum([portions[i] for i in free]), rest
        for i in free:
            addition = min(reach - holding[i], max(1, remaining * portions[i] // pool), rest)
            holding[i] = holding[i] + addition
            rest = rest - addition
    return np.array([reach] + holding)


def ragged_sizes(stream_key, amount, total, most, slope):
    if amount == 2:
        one = jax.random.randint(stream_key, (), max(1, total - most), min(most, total - 1) + 1)
        return jnp.stack([one, total - one])
    lengths = jnp.asarray(split_up(amount, total, most, slope), jnp.int32)
    couples = (amount - 1) // 2
    donor, receiver = lengths[1:1 + 2 * couples:2], lengths[2:2 + 2 * couples:2]
    room = jnp.minimum(donor - 1, most - receiver)
    shifted = jax.random.randint(jax.random.fold_in(stream_key, 1), (couples,), 0, 1 << 20) % (room + 1)
    lengths = lengths.at[1:1 + 2 * couples:2].set(donor - shifted).at[2:2 + 2 * couples:2].set(receiver + shifted)
    return lengths[jax.random.permutation(jax.random.fold_in(stream_key, 2), amount)]


def noise(stream_key, extent, scale, reach, cuts=(), kind=jnp.bfloat16):
    values = jax.random.normal(stream_key, extent, jnp.float32) * scale
    if len(cuts) > 0:
        values = block_levels(stream_key, extent, cuts, -0.22, 0.18) * values
    return jnp.clip(values, min=-reach, max=reach).astype(kind)


def setup_inputs(seed: int = 0) -> dict:
    seeds = jax.random.split(jax.random.key(seed), 7)
    return {
        "displacement": noise(seeds[0], (3, NZ, NODES), 1.0, 6.0, ((1, 32),), jnp.float32),
        "macro_modulus": jnp.clip(jnp.exp(math.log(4.0) - 2.0794415 * jax.random.uniform(seeds[1], (8, ELEMS), jnp.float32) ** block_levels(seeds[1], (8, ELEMS), ((1, 32),), -0.2, 0.2)), 0.5, 4.0),
        "damaged_count": ragged_sizes(seeds[2], DOMAINS, DMG_SUM, DMG_DEV, 2).astype(jnp.int32),
        "damaged_points": draw_damaged_points(jax.random.fold_in(seeds[6], 71), 0),
        "damage": jnp.clip(0.59765625 * jax.random.uniform(seeds[4], (SLOTS, VOX), jnp.float32) ** block_levels(seeds[4], (SLOTS, VOX), ((0, 32),), -0.2, 0.2), 0.0, 0.59765625).astype(jnp.bfloat16),
        "voxel_modulus": jnp.clip(jnp.exp(math.log(4.0) - 2.0794415 * jax.random.uniform(seeds[5], (SLOTS, VOX), jnp.float32) ** block_levels(seeds[5], (SLOTS, VOX), ((0, 32),), -0.2, 0.2)), 0.5, 4.0).astype(jnp.bfloat16),
    }


lam_hat = 0.2 / 0.72
mu_hat = 1.0 / 2.4
ref_modulus = 2.0
kappa_sq = 4.0
voigt_pairs = ((0, 0), (1, 1), (2, 2), (1, 2), (0, 2), (0, 1))

def shape_table():
    gauss_coord = 1.0 / math.sqrt(3.0)
    gradients = np.zeros((8, 8, 3), np.float32)
    for corner in range(8):
        corner_signs = [2 * (corner >> axis_no & 1) - 1 for axis_no in range(3)]
        for gauss_no in range(8):
            gauss_coords = [(2 * (gauss_no >> axis_no & 1) - 1) * gauss_coord for axis_no in range(3)]
            factor = [(1.0 + corner_signs[axis_no] * gauss_coords[axis_no]) / 2.0 for axis_no in range(3)]
            for direction in range(3):
                entry_value = float(corner_signs[direction])
                for other_dir in range(3):
                    if other_dir != direction:
                        entry_value = entry_value * factor[other_dir]
                gradients[corner, gauss_no, direction] = entry_value
    return gradients

def element_strain(node_grid, layers, side):
    gradients = jnp.asarray(shape_table())
    corner_list = []
    for corner in range(8):
        off_x, off_y, off_z = (corner & 1, corner >> 1 & 1, corner >> 2 & 1)
        piece = node_grid[:, off_z:off_z + layers, off_y:off_y + side, off_x:off_x + side]
        corner_list.append(piece.reshape(3, layers * side * side))
    stacked = jnp.stack(corner_list)
    displ_grad = jnp.einsum('cie,cqj->ijqe', stacked, gradients, precision=lax.Precision.HIGHEST)
    return jnp.stack([0.5 * (displ_grad[first_dim, second_dim] + displ_grad[second_dim, first_dim]) for first_dim, second_dim in voigt_pairs])

def nodal_forces(stress, layers, side):
    gradients = jnp.asarray(shape_table())
    tensor = jnp.stack([jnp.stack([stress[0], stress[5], stress[4]]), jnp.stack([stress[5], stress[1], stress[3]]), jnp.stack([stress[4], stress[3], stress[2]])])
    contrib = 0.125 * jnp.einsum('ijqe,cqj->cie', tensor, gradients, precision=lax.Precision.HIGHEST)
    node_grid = jnp.zeros((3, layers + 1, side + 1, side + 1), jnp.float32)
    for corner in range(8):
        off_x, off_y, off_z = (corner & 1, corner >> 1 & 1, corner >> 2 & 1)
        node_grid = node_grid.at[:, off_z:off_z + layers, off_y:off_y + side, off_x:off_x + side].add(contrib[corner].reshape(3, layers, side, side))
    return node_grid

def elastic_list(components, modulus):
    trace_sum = components[0] + components[1] + components[2]
    result = []
    for comp in range(6):
        inner = 2.0 * mu_hat * components[comp]
        if comp < 3:
            inner = inner + lam_hat * trace_sum
        result.append(modulus * inner)
    return result

def voxel_update(components, old_damage, modulus):
    energy = components[0] ** 2 + components[1] ** 2 + components[2] ** 2 + 2.0 * (components[3] ** 2 + components[4] ** 2 + components[5] ** 2)
    damage_now = jnp.maximum(old_damage, energy / (energy + kappa_sq))
    stress = elastic_list(components, (1.0 - damage_now) * modulus)
    medium = elastic_list(components, ref_modulus)
    polarization = [stress[comp] - medium[comp] for comp in range(6)]
    return (stress, polarization, damage_now)

def green_apply(components, freq_x, freq_y, freq_z):
    wave_vec = (freq_x, freq_y, freq_z)
    square = freq_x * freq_x + freq_y * freq_y + freq_z * freq_z
    inverse = jnp.where(square > 0.5, 1.0 / jnp.maximum(square, 1.0), 0.0)
    tensor = ((components[0], components[5], components[4]), (components[5], components[1], components[3]), (components[4], components[3], components[2]))
    traction = [tensor[row_no][0] * freq_x + tensor[row_no][1] * freq_y + tensor[row_no][2] * freq_z for row_no in range(3)]
    along_wave = freq_x * traction[0] + freq_y * traction[1] + freq_z * traction[2]
    lam_ref = ref_modulus * lam_hat
    mu_ref = ref_modulus * mu_hat
    coupling = (lam_ref + mu_ref) / (mu_ref * (lam_ref + 2.0 * mu_ref))
    amplitude = [inverse * traction[row_no] / mu_ref - coupling * along_wave * inverse * inverse * wave_vec[row_no] for row_no in range(3)]
    return [0.5 * (wave_vec[first_dim] * amplitude[second_dim] + wave_vec[second_dim] * amplitude[first_dim]) for first_dim, second_dim in voigt_pairs]

def narrow(values):
    return lax.optimization_barrier(values.astype(jnp.bfloat16)).astype(jnp.float32)

def cell_block(macro, old_damage, modulus):
    cell_side = CELL
    cell_total = old_damage.shape[0]
    steps_index = jnp.arange(cell_side).astype(jnp.int32)
    signed = jnp.where(steps_index < cell_side // 2, steps_index, steps_index - cell_side).astype(jnp.float32)
    freq_x = signed[None, :, None, None]
    freq_y = signed[None, None, :, None]
    freq_z = jnp.arange(cell_side // 2 + 1).astype(jnp.float32)[None, None, None, :]
    strain_now = jnp.broadcast_to(macro[:, :, None], (cell_total, 6, VOX))
    for sweep_no in range(SWEEPS):
        components = [strain_now[:, comp] for comp in range(6)]
        stress, polarization, damage_now = voxel_update(components, old_damage, modulus)
        spectra = [jnp.fft.rfftn(narrow(part_field).reshape(cell_total, cell_side, cell_side, cell_side), axes=(1, 2, 3)) for part_field in polarization]
        real_green = green_apply([spectrum.real for spectrum in spectra], freq_x, freq_y, freq_z)
        imag_green = green_apply([spectrum.imag for spectrum in spectra], freq_x, freq_y, freq_z)
        back = [jnp.fft.irfftn(narrow(real_green[comp]) + 1j * narrow(imag_green[comp]), s=(cell_side, cell_side, cell_side), axes=(1, 2, 3)).reshape(cell_total, VOX) for comp in range(6)]
        strain_now = jnp.stack([macro[:, comp:comp + 1] - back[comp] for comp in range(6)], axis=1)
    components = [strain_now[:, comp] for comp in range(6)]
    stress, polarization, damage_now = voxel_update(components, old_damage, modulus)
    mean_stress = jnp.stack([lax.optimization_barrier(jnp.mean(stress[comp], axis=1)) for comp in range(6)], axis=1)
    return (damage_now, mean_stress)

def reference(displacement, macro_modulus, damaged_count, damaged_points, damage, voxel_modulus):
    part_total = damaged_count.shape[0]
    layers = displacement.shape[1]
    base_layer = jnp.zeros((3, 1, displacement.shape[2]), displacement.dtype)
    node_grid = jnp.concatenate([base_layer, displacement], axis=1).reshape(3, layers + 1, EXY + 1, EXY + 1)
    macro_strain = element_strain(node_grid, layers, EXY)
    elem_total = macro_strain.shape[2]
    elastic_stress = jnp.stack(elastic_list([macro_strain[comp] for comp in range(6)], macro_modulus)).reshape(6, 8 * elem_total)
    flat_strain = macro_strain.reshape(6, 8 * elem_total)
    per_part = LZ * EXY * EXY
    slot_index = jnp.arange(DMG_DEV).astype(jnp.int32)
    is_live = (slot_index[None, :] < damaged_count[:, None]).reshape(-1)
    gauss_no = damaged_points // per_part
    element = jnp.arange(part_total).astype(jnp.int32)[:, None] * per_part + damaged_points % per_part
    column = (gauss_no * elem_total + element).astype(jnp.int32).reshape(-1)
    cell_strain = flat_strain[:, column].T.astype(jnp.bfloat16)

    def per_partition(inputs):
        macro, old_damage, modulus = inputs
        return cell_block(macro.astype(jnp.float32), old_damage.astype(jnp.float32), modulus.astype(jnp.float32))
    new_dmg, cell_stress = lax.map(per_partition, (cell_strain.reshape(part_total, DMG_DEV, 6), damage.reshape(part_total, DMG_DEV, VOX), voxel_modulus.reshape(part_total, DMG_DEV, VOX)))
    new_damage = jnp.where(is_live[:, None], new_dmg.reshape(SLOTS, VOX).astype(jnp.bfloat16), damage)
    cell_rounded = cell_stress.reshape(SLOTS, 6).astype(jnp.bfloat16).astype(jnp.float32)
    target = jnp.where(is_live, column, 8 * elem_total).astype(jnp.int32)
    point_stress = elastic_stress.at[:, target].set(cell_rounded.T, mode='drop')
    force_grid = nodal_forces(point_stress.reshape(6, 8, elem_total), layers, EXY)
    nodal_force = force_grid[:, 1:].reshape(3, layers, (EXY + 1) * (EXY + 1))
    return (nodal_force, new_damage)
```

```python
import math

import jax
import jax.numpy as jnp
import numpy as np
from jax import lax
from jax.experimental import pallas as pl
from jax.experimental.pallas import tpu as pltpu
from jax.sharding import PartitionSpec as P

CELL = 16
PLANE = CELL * CELL
VOX = CELL**3
EXY = 16
NODES = (EXY + 1) ** 2
NODE_PAD = 384
HALF = 128
ROWS = 16

lam_hat = 0.2 / 0.72
mu_hat = 1.0 / 2.4
ref_modulus = 2.0
kappa_sq = 4.0
voigt_pairs = ((0, 0), (1, 1), (2, 2), (1, 2), (0, 2), (0, 1))
packed = {}
for _a in range(6):
    for _b in range(_a, 6):
        packed[(_a, _b)] = packed[(_b, _a)] = len(packed) - sum(
            1 for _p in packed if _p[0] > _p[1]
        )
C1, C2, C3 = (math.cos(math.pi * n / 8) for n in (1, 2, 3))
f32, bf16 = jnp.float32, jnp.bfloat16
HIGHEST = lax.Precision.HIGHEST


def shifted(value, axis, steps):
    count = lax.axis_size(axis)
    initial, last = (max(0, -steps), min(count, count - steps))
    return lax.ppermute(value, axis, [(source, source + steps) for source in range(initial, last)])


def shape_table():
    gauss_coord = 1.0 / math.sqrt(3.0)
    gradients = np.zeros((8, 8, 3))
    for corner in range(8):
        signs = [2 * (corner >> d & 1) - 1 for d in range(3)]
        for gauss_no in range(8):
            coords = [(2 * (gauss_no >> d & 1) - 1) * gauss_coord for d in range(3)]
            factor = [(1.0 + signs[d] * coords[d]) / 2.0 for d in range(3)]
            for d in range(3):
                value = float(signs[d])
                for other in range(3):
                    if other != d:
                        value *= factor[other]
                gradients[corner, gauss_no, d] = value
    return gradients


def macro_tables():
    table = shape_table()
    to_strain = np.zeros((48, 32))
    to_force = np.zeros((32, 48))
    for corner in range(8):
        base = (corner & 3) * 8 + (corner >> 2) * 3
        for k, (a, b) in enumerate(voigt_pairs):
            for q in range(8):
                to_strain[k * 8 + q, base + a] += 0.5 * table[corner, q, b]
                to_strain[k * 8 + q, base + b] += 0.5 * table[corner, q, a]
                to_force[base + a, k * 8 + q] += 0.125 * table[corner, q, b]
                if a != b:
                    to_force[base + b, k * 8 + q] += 0.125 * table[corner, q, a]
    pick = np.zeros((NODE_PAD, 4 * EXY * EXY))
    for cy in range(2):
        for cx in range(2):
            for y in range(EXY):
                for x in range(EXY):
                    column = (2 * cy + cx) * EXY * EXY + y * EXY + x
                    pick[(y + cy) * (EXY + 1) + x + cx, column] = 1.0
    return to_strain, to_force, pick


def green_matrix(nx, ny, nz):
    n = np.stack(np.broadcast_arrays(nx, ny, nz)).astype(np.float64)
    square = (n * n).sum(0)
    inverse = np.where(square > 0.5, 1.0 / np.maximum(square, 1.0), 0.0)
    lam_ref, mu_ref = ref_modulus * lam_hat, ref_modulus * mu_hat
    coupling = (lam_ref + mu_ref) / (mu_ref * (lam_ref + 2.0 * mu_ref))
    out = np.zeros((6, 6) + square.shape)
    for column, (a, b) in enumerate(voigt_pairs):
        traction = np.zeros_like(n)
        traction[a] += n[b]
        if a != b:
            traction[b] += n[a]
        along = (n * traction).sum(0)
        amplitude = inverse * traction / mu_ref - coupling * along * inverse * inverse * n
        for k, (c, d) in enumerate(voigt_pairs):
            out[k, column] = 0.5 * (n[c] * amplitude[d] + n[d] * amplitude[c])
    return out


def effective_green():
    index = np.arange(CELL)
    signed = np.where(index < CELL // 2, index, index - CELL)
    mirror = (-index) % CELL
    half = CELL // 2
    fx, fy = signed[:, None, None], signed[None, :, None]
    given = green_matrix(fx, fy, np.arange(half + 1)[None, None, :])
    turned = given[:, :, mirror][:, :, :, mirror]
    full = np.zeros((6, 6, CELL, CELL, CELL))
    full[..., : half + 1] = given
    for plane in (0, half):
        full[..., plane] = 0.5 * (given[..., plane] + turned[..., plane])
    for plane in range(half + 1, CELL):
        full[..., plane] = turned[..., CELL - plane]
    full[:, 3:] *= 0.5
    return full[:, :, : half + 1].reshape(6, 6, half + 1, PLANE)


def cell_tables():
    green = effective_green()
    coefs = np.zeros((9, 24, PLANE))
    for a in range(6):
        for b in range(a, 6):
            coefs[:, packed[(a, b)]] = green[a, b]
    wide = green.transpose(2, 1, 0, 3).reshape(9, 6, 6 * PLANE)
    upper = wide.astype(bf16).astype(np.float64)
    first = np.zeros((9, 32, 6 * PLANE))
    first[:, 0:6] = upper
    first[:, 6:12] = upper
    first[:, 12:18] = wide - upper
    place = np.arange(PLANE)
    phase = (place // CELL)[:, None] * (place // CELL)[None, :] + (place % CELL)[:, None] * (
        place % CELL
    )[None, :]
    angle = (phase % CELL) * (2.0 * math.pi / CELL)
    cos, sin = np.cos(angle), np.sin(angle)
    forward = np.block([[cos, sin], [-sin, cos]])
    inverse = np.block([[cos, -sin], [sin, cos]]) * (2.0 / VOX)
    return coefs, first, forward, inverse, cos + sin, (cos + sin) / VOX


def parts3(value):
    first = value.astype(bf16)
    rest = value - first.astype(f32)
    second = rest.astype(bf16)
    third = (rest - second.astype(f32)).astype(bf16)
    return jnp.concatenate([first, second, third], axis=0)


def total3(value):
    rows = value.shape[0] // 3
    return value[:rows] + value[rows : 2 * rows] + value[2 * rows :]


def forward_x(v):
    s = [v[x] + v[x + 8] for x in range(8)]
    d = [v[x] - v[x + 8] for x in range(8)]
    a = [s[x] + s[x + 4] for x in range(4)]
    b = [s[x] - s[x + 4] for x in range(4)]
    a02, a13 = a[0] + a[2], a[1] + a[3]
    bm, bp = C2 * (b[1] - b[3]), C2 * (b[1] + b[3])
    p1, p2, p3 = d[1] - d[7], C2 * (d[2] - d[6]), d[3] - d[5]
    q1, q2, q3 = d[1] + d[7], C2 * (d[2] + d[6]), d[3] + d[5]
    re_sum, re_dif = d[0] + p2, d[0] - p2
    re_a, re_b = C1 * p1 + C3 * p3, C3 * p1 - C1 * p3
    im_sum, im_dif = q2 + d[4], q2 - d[4]
    im_a, im_b = C3 * q1 + C1 * q3, C1 * q1 - C3 * q3
    pairs = [
        (re_sum + re_a, im_a + im_sum),
        (b[0] + bm, bp + b[2]),
        (re_dif + re_b, im_b + im_dif),
        (a[0] - a[2], a[1] - a[3]),
        (re_dif - re_b, im_b - im_dif),
        (b[0] - bm, bp - b[2]),
        (re_sum - re_a, im_a - im_sum),
    ]
    return a02 + a13, a02 - a13, pairs


def inverse_x(x0, x8, pairs):
    r = [None] + [pair[0] for pair in pairs]
    m = [None] + [pair[1] for pair in pairs]
    plus, minus = x0 + x8, x0 - x8
    r26p, r26m = r[2] + r[6], C2 * (r[2] - r[6])
    p4 = plus + r[4]
    even = [p4 + r26p, minus + r26m, plus - r[4], minus - r26m, p4 - r26p]
    r17p, r17m, r35p, r35m = r[1] + r[7], r[1] - r[7], r[3] + r[5], r[3] - r[5]
    odd = [r17p + r35p, C1 * r17m + C3 * r35m, C2 * (r17p - r35p), C3 * r17m - C1 * r35m]
    cosine = [None] * 9
    for x in range(4):
        cosine[x] = even[x] + odd[x]
        cosine[8 - x] = even[x] - odd[x]
    cosine[4] = even[4]
    m26p = C2 * (m[2] + m[6])
    s_even = [None, m26p + m[4], m[2] - m[6], m26p - m[4]]
    m17p, m17m, m35p, m35m = m[1] + m[7], m[1] - m[7], m[3] + m[5], m[3] - m[5]
    s_odd = [None, C3 * m17p + C1 * m35p, C2 * (m17m + m35m), C1 * m17p - C3 * m35p]
    sine = [None] * 8
    for x in range(1, 4):
        sine[x] = s_odd[x] + s_even[x]
        sine[8 - x] = s_odd[x] - s_even[x]
    sine[4] = m17m - m35m
    out = [None] * 16
    out[0], out[8] = cosine[0], cosine[8]
    for x in range(1, 8):
        out[x] = cosine[x] + sine[x]
        out[16 - x] = cosine[x] - sine[x]
    return out


def damage_of(e):
    energy = e[0] * e[0] + e[1] * e[1] + e[2] * e[2]
    energy = energy + 2.0 * (e[3] * e[3] + e[4] * e[4] + e[5] * e[5])
    return energy / (energy + kappa_sq)


def unit_law(e, shear):
    volume = lam_hat * (e[0] + e[1] + e[2])
    return [2.0 * mu_hat * e[k] + volume for k in range(3)] + [
        (shear * 2.0 * mu_hat) * e[k] for k in range(3, 6)
    ]


def kernel(
    layers,
    slots,
    count_ref,
    nodes_ref,
    modulus_ref,
    points_ref,
    damage_ref,
    voxel_ref,
    strain_tab,
    force_tab,
    pick_tab,
    coef_tab,
    first_tab,
    forward_tab,
    inverse_tab,
    real_forward,
    real_inverse,
    force_ref,
    new_ref,
    field,
    spec_c,
    spec_r,
    back_c,
    back_r,
    freq,
    green,
    macro,
    stress_s,
    acc,
):
    elems = layers * EXY * EXY
    chunks = slots // ROWS
    count = count_ref[0]

    spread = total3(jnp.dot(parts3(nodes_ref[...]), pick_tab[...], preferred_element_type=f32))
    plane = EXY * EXY
    corners = jnp.concatenate(
        [
            jnp.concatenate(
                [spread[z * 8 : z * 8 + 8, c * plane : (c + 1) * plane] for z in range(layers)],
                axis=1,
            )
            for c in range(4)
        ],
        axis=0,
    )
    strain = jnp.dot(strain_tab[...], corners, precision=HIGHEST, preferred_element_type=f32)
    modulus = modulus_ref[...]
    law = unit_law([strain[k * 8 : k * 8 + 8] for k in range(6)], 1.0)
    stress = jnp.concatenate([modulus * law[k] for k in range(6)], axis=0)
    stress_s[...] = stress

    points = points_ref[...]
    element = points % elems
    gauss = points // elems
    hot = (lax.broadcasted_iota(jnp.int32, (slots, elems), 1) == element).astype(f32).astype(bf16)
    both = parts3(jnp.concatenate([strain, stress], axis=0))
    picked = lax.dot_general(hot, both, (((1,), (1,)), ((), ())), preferred_element_type=f32)
    picked = picked[:, 0:96] + picked[:, 96:192] + picked[:, 192:288]
    lane96 = lax.broadcasted_iota(jnp.int32, (slots, 96), 1)
    own = [
        jnp.sum(jnp.where(lane96 == k * 8 + gauss, picked, 0.0), axis=1, keepdims=True)
        for k in range(12)
    ]
    mean = [own[k].astype(bf16).astype(f32) for k in range(6)]
    for k in range(6):
        macro[k] = jnp.broadcast_to(mean[k], (slots, HALF))

    mean_law = unit_law(mean, 2.0)
    mean_damage = damage_of(mean)
    lane32 = lax.broadcasted_iota(jnp.int32, (slots, 32), 1)
    upper = jnp.zeros((slots, 32), f32)
    for k in range(6):
        high = mean_law[k].astype(bf16).astype(f32)
        upper = jnp.where((lane32 == k) | (lane32 == 12 + k), high, upper)
        upper = jnp.where(lane32 == 6 + k, mean_law[k] - high, upper)
    mean_parts = upper.astype(bf16)
    for r in range(chunks):
        rows = slice(r * ROWS, (r + 1) * ROWS)
        for h in range(2):
            lanes = slice(h * HALF, (h + 1) * HALF)
            scalar = []
            for x in range(CELL):
                cols = slice(x * PLANE + h * HALF, x * PLANE + (h + 1) * HALF)
                old = damage_ref[rows, cols].astype(f32)
                young = voxel_ref[rows, cols].astype(f32)
                scalar.append((1.0 - jnp.maximum(old, mean_damage[rows])) * young - ref_modulus)
            x0, x8, pairs = forward_x(scalar)
            spec_r[0, rows, lanes] = x0.astype(bf16)
            spec_r[1, rows, lanes] = x8.astype(bf16)
            for j in range(7):
                spec_c[j, rows, h * HALF : (h + 1) * HALF] = pairs[j][0].astype(bf16)
                spec_c[j, rows, PLANE + h * HALF : PLANE + (h + 1) * HALF] = pairs[j][1].astype(
                    bf16
                )

    def first_c(j, carry):
        spectrum = jnp.dot(spec_c[j, 0:slots], forward_tab[...], preferred_element_type=f32)
        weight = jnp.dot(mean_parts, first_tab[j + 1], preferred_element_type=f32)
        for k in range(6):
            part = weight[:, k * PLANE : (k + 1) * PLANE]
            rows = slice(k * slots, (k + 1) * slots)
            green[rows, 0:PLANE] = (part * spectrum[:, 0:PLANE]).astype(bf16)
            green[rows, PLANE:] = (part * spectrum[:, PLANE:]).astype(bf16)
        back_c[j] = jnp.dot(green[...], inverse_tab[...], preferred_element_type=f32)
        return carry

    def first_r(j, carry):
        spectrum = jnp.dot(spec_r[j, 0:slots], real_forward[...], preferred_element_type=f32)
        weight = jnp.dot(mean_parts, first_tab[j * 8], preferred_element_type=f32)
        for k in range(6):
            part = weight[:, k * PLANE : (k + 1) * PLANE]
            green[k * slots : (k + 1) * slots, 0:PLANE] = (part * spectrum).astype(bf16)
        back_r[j] = jnp.dot(green[:, 0:PLANE], real_inverse[...], preferred_element_type=f32)
        return carry

    def to_strain(k, carry):
        for r in range(chunks):
            rows = pl.ds(pl.multiple_of(k * slots + r * ROWS, ROWS), ROWS)
            base = macro[k, r * ROWS : (r + 1) * ROWS]
            for h in range(2):
                lanes = slice(h * HALF, (h + 1) * HALF)
                upper_lanes = slice(PLANE + h * HALF, PLANE + (h + 1) * HALF)
                pairs = [(back_c[j, rows, lanes], back_c[j, rows, upper_lanes]) for j in range(7)]
                values = inverse_x(back_r[0, rows, lanes], back_r[1, rows, lanes], pairs)
                for x in range(CELL):
                    field[k * CELL + x, r * ROWS : (r + 1) * ROWS, lanes] = base - values[x]
        return carry

    lax.fori_loop(0, 7, first_c, 0)
    lax.fori_loop(0, 2, first_r, 0)
    lax.fori_loop(0, 6, to_strain, 0)

    def polarize(x, carry):
        cols = pl.ds(pl.multiple_of(x * PLANE, PLANE), PLANE)
        for r in range(chunks):
            rows = slice(r * ROWS, (r + 1) * ROWS)
            e = [field[k * CELL + x, rows] for k in range(6)]
            old = damage_ref[rows, cols].astype(f32)
            young = voxel_ref[rows, cols].astype(f32)
            change = (1.0 - jnp.maximum(old, damage_of(e))) * young - ref_modulus
            for k, unit in enumerate(unit_law(e, 2.0)):
                field[k * CELL + x, rows] = change * unit
        return carry

    def to_spectrum(k, carry):
        for r in range(chunks):
            rows = pl.ds(pl.multiple_of(k * slots + r * ROWS, ROWS), ROWS)
            for h in range(2):
                lanes = slice(h * HALF, (h + 1) * HALF)
                upper_lanes = slice(PLANE + h * HALF, PLANE + (h + 1) * HALF)
                x0, x8, pairs = forward_x(
                    [field[k * CELL + x, r * ROWS : (r + 1) * ROWS, lanes] for x in range(CELL)]
                )
                spec_r[0, rows, lanes] = x0.astype(bf16)
                spec_r[1, rows, lanes] = x8.astype(bf16)
                for j in range(7):
                    spec_c[j, rows, lanes] = pairs[j][0].astype(bf16)
                    spec_c[j, rows, upper_lanes] = pairs[j][1].astype(bf16)
        return carry

    def apply_green(index, planes):
        for h in range(2):
            lanes = slice(h * HALF, (h + 1) * HALF)
            coefs = [
                jnp.broadcast_to(coef_tab[index, c : c + 1, lanes], (ROWS, HALF))
                for c in range(21)
            ]
            for part in range(planes):
                where = slice(part * PLANE + h * HALF, part * PLANE + (h + 1) * HALF)
                for r in range(chunks):
                    t = [
                        freq[k * slots + r * ROWS : k * slots + (r + 1) * ROWS, where]
                        for k in range(6)
                    ]
                    for k in range(6):
                        total = coefs[packed[(k, 0)]] * t[0]
                        for b in range(1, 6):
                            total = total + coefs[packed[(k, b)]] * t[b]
                        green[k * slots + r * ROWS : k * slots + (r + 1) * ROWS, where] = (
                            total.astype(bf16)
                        )

    def second_c(j, carry):
        freq[...] = jnp.dot(spec_c[j], forward_tab[...], preferred_element_type=f32)
        apply_green(j + 1, 2)
        back_c[j] = jnp.dot(green[...], inverse_tab[...], preferred_element_type=f32)
        return carry

    def second_r(j, carry):
        freq[:, 0:PLANE] = jnp.dot(spec_r[j], real_forward[...], preferred_element_type=f32)
        apply_green(j * 8, 1)
        back_r[j] = jnp.dot(green[:, 0:PLANE], real_inverse[...], preferred_element_type=f32)
        return carry

    lax.fori_loop(0, CELL, polarize, 0)
    lax.fori_loop(0, 6, to_spectrum, 0)
    lax.fori_loop(0, 7, second_c, 0)
    lax.fori_loop(0, 2, second_r, 0)
    lax.fori_loop(0, 6, to_strain, 0)

    for r in range(chunks):
        rows = slice(r * ROWS, (r + 1) * ROWS)
        live = lax.broadcasted_iota(jnp.int32, (ROWS, PLANE), 0) + r * ROWS < count

        def finish(x, sums, rows=rows, live=live):
            cols = pl.ds(pl.multiple_of(x * PLANE, PLANE), PLANE)
            e = [field[k * CELL + x, rows] for k in range(6)]
            old = damage_ref[rows, cols].astype(f32)
            young = voxel_ref[rows, cols].astype(f32)
            now = jnp.maximum(old, damage_of(e))
            new_ref[rows, cols] = jnp.where(live, now, old).astype(bf16)
            left = (1.0 - now) * young
            out = []
            for k, unit in enumerate(unit_law(e, 1.0)):
                value = left * unit
                out.append(sums[k] + (value[:, 0:HALF] + value[:, HALF:]))
            return tuple(out)

        sums = lax.fori_loop(0, CELL, finish, (jnp.zeros((ROWS, HALF), f32),) * 6)
        for k in range(6):
            acc[k, rows] = sums[k]

    alive = lax.broadcasted_iota(jnp.int32, (slots, 1), 0) < count
    lane128 = lax.broadcasted_iota(jnp.int32, (slots, HALF), 1)
    change = jnp.zeros((slots, HALF), f32)
    for k in range(6):
        cell_mean = jnp.sum(acc[k], axis=1, keepdims=True) * (1.0 / VOX)
        delta = jnp.where(alive, cell_mean.astype(bf16).astype(f32) - own[6 + k], 0.0)
        change = jnp.where(lane128 == k * 8 + gauss, delta, change)
    turned = jnp.transpose(change)[0:48]
    stress = stress_s[...] + total3(jnp.dot(parts3(turned), hot, preferred_element_type=f32))
    contrib = jnp.dot(force_tab[...], stress, precision=HIGHEST, preferred_element_type=f32)
    by_layer = jnp.concatenate(
        [
            jnp.concatenate(
                [contrib[c * 8 : c * 8 + 8, z * plane : (z + 1) * plane] for c in range(4)], axis=1
            )
            for z in range(layers)
        ],
        axis=0,
    )
    force_ref[...] = total3(
        lax.dot_general(
            parts3(by_layer), pick_tab[...], (((1,), (1,)), ((), ())), preferred_element_type=f32
        )
    )


def run_kernel(count, nodes, modulus, points, damage, voxel, layers, interpret=False):
    slots = damage.shape[0]
    to_strain, to_force, pick = macro_tables()
    coefs, first, forward, inverse, real_forward, real_inverse = cell_tables()
    consts = (
        jnp.asarray(to_strain, f32),
        jnp.asarray(to_force, f32),
        jnp.asarray(pick, bf16),
        jnp.asarray(coefs, f32),
        jnp.asarray(first, bf16),
        jnp.asarray(forward, bf16),
        jnp.asarray(inverse, bf16),
        jnp.asarray(real_forward, bf16),
        jnp.asarray(real_inverse, bf16),
    )
    vmem = pl.BlockSpec(memory_space=pltpu.VMEM)
    rows = 6 * slots

    def body(*refs):
        kernel(layers, slots, *refs)

    return pl.pallas_call(
        body,
        out_shape=(
            jax.ShapeDtypeStruct((layers * 8, NODE_PAD), f32),
            jax.ShapeDtypeStruct(damage.shape, bf16),
        ),
        in_specs=[pl.BlockSpec(memory_space=pltpu.SMEM)] + [vmem] * 14,
        out_specs=(vmem, vmem),
        scratch_shapes=[
            pltpu.VMEM((6 * CELL, slots, PLANE), f32),
            pltpu.VMEM((7, rows, 2 * PLANE), bf16),
            pltpu.VMEM((2, rows, PLANE), bf16),
            pltpu.VMEM((7, rows, 2 * PLANE), f32),
            pltpu.VMEM((2, rows, PLANE), f32),
            pltpu.VMEM((rows, 2 * PLANE), f32),
            pltpu.VMEM((rows, 2 * PLANE), bf16),
            pltpu.VMEM((6, slots, HALF), f32),
            pltpu.VMEM((48, layers * EXY * EXY), f32),
            pltpu.VMEM((6, slots, HALF), f32),
        ],
        compiler_params=pltpu.CompilerParams(vmem_limit_bytes=44 * 1024 * 1024),
        cost_estimate=pl.CostEstimate(flops=10**10, bytes_accessed=8 * 10**6, transcendentals=0),
        interpret=interpret,
    )(count, nodes, modulus, points, damage, voxel, *consts)


def body(displacement, macro_modulus, damaged_count, damaged_points, damage, voxel_modulus):
    layers = displacement.shape[1]
    axes = ("dom", "sub")
    below = shifted(displacement[:, layers - 1 :], axes, 1)
    grid = jnp.concatenate([below, displacement], axis=1)
    nodes = jnp.stack([grid[:, :layers], grid[:, 1:]]).transpose(2, 0, 1, 3)
    nodes = nodes.reshape(layers, 6, NODES)
    nodes = jnp.pad(nodes, ((0, 0), (0, 2), (0, NODE_PAD - NODES))).reshape(layers * 8, NODE_PAD)
    force, new_damage = run_kernel(
        damaged_count,
        nodes,
        macro_modulus,
        damaged_points.reshape(-1, 1),
        damage,
        voxel_modulus,
        layers,
    )
    force = force.reshape(layers, 8, NODE_PAD)[:, :, :NODES]
    from_above = shifted(force[:1, 0:3], axes, -1)
    lower = jnp.concatenate([force[1:, 0:3], from_above], axis=0)
    own_forces = (force[:, 3:6] + lower).transpose(1, 0, 2)
    return (own_forces, new_damage)


def solution(mesh):
    return jax.shard_map(
        body,
        mesh=mesh,
        in_specs=(
            P(None, ("dom", "sub"), None),
            P(None, ("dom", "sub")),
            P(("dom", "sub")),
            P(("dom", "sub"), None),
            P(("dom", "sub"), None),
            P(("dom", "sub"), None),
        ),
        out_specs=(P(None, ("dom", "sub"), None), P(("dom", "sub"), None)),
        check_vma=False,
    )
```

```python
import functools
import math

import jax
import jax.numpy as jnp
import numpy as np
from jax import lax
from jax.experimental import pallas as pl
from jax.experimental.pallas import tpu as pltpu
from jax.sharding import PartitionSpec as P

CELL = 16
PLANE = CELL * CELL
VOX = CELL**3
EXY = 16
NODES = (EXY + 1) ** 2
NODE_PAD = 384
HALF = 128
ROWS = 16

lam_hat = 0.2 / 0.72
mu_hat = 1.0 / 2.4
ref_modulus = 2.0
kappa_sq = 4.0
voigt_pairs = ((0, 0), (1, 1), (2, 2), (1, 2), (0, 2), (0, 1))
packed = {}
for _a in range(6):
    for _b in range(_a, 6):
        packed[(_a, _b)] = packed[(_b, _a)] = len(packed) - sum(
            1 for _p in packed if _p[0] > _p[1]
        )
C1, C2, C3 = (math.cos(math.pi * n / 8) for n in (1, 2, 3))
f32, bf16 = jnp.float32, jnp.bfloat16
MESH = pl.DeviceIdType.MESH
HIGHEST = lax.Precision.HIGHEST


def shape_table():
    gauss_coord = 1.0 / math.sqrt(3.0)
    gradients = np.zeros((8, 8, 3))
    for corner in range(8):
        signs = [2 * (corner >> d & 1) - 1 for d in range(3)]
        for gauss_no in range(8):
            coords = [(2 * (gauss_no >> d & 1) - 1) * gauss_coord for d in range(3)]
            factor = [(1.0 + signs[d] * coords[d]) / 2.0 for d in range(3)]
            for d in range(3):
                value = float(signs[d])
                for other in range(3):
                    if other != d:
                        value *= factor[other]
                gradients[corner, gauss_no, d] = value
    return gradients


def macro_tables():
    table = shape_table()
    to_strain = np.zeros((48, 32))
    to_force = np.zeros((32, 48))
    for corner in range(8):
        base = (corner & 3) * 8 + (corner >> 2) * 3
        for k, (a, b) in enumerate(voigt_pairs):
            for q in range(8):
                to_strain[k * 8 + q, base + a] += 0.5 * table[corner, q, b]
                to_strain[k * 8 + q, base + b] += 0.5 * table[corner, q, a]
                to_force[base + a, k * 8 + q] += 0.125 * table[corner, q, b]
                if a != b:
                    to_force[base + b, k * 8 + q] += 0.125 * table[corner, q, a]
    pick = np.zeros((NODE_PAD, 4 * EXY * EXY))
    for cy in range(2):
        for cx in range(2):
            for y in range(EXY):
                for x in range(EXY):
                    column = (2 * cy + cx) * EXY * EXY + y * EXY + x
                    pick[(y + cy) * (EXY + 1) + x + cx, column] = 1.0
    return to_strain, to_force, pick


def green_matrix(nx, ny, nz):
    n = np.stack(np.broadcast_arrays(nx, ny, nz)).astype(np.float64)
    square = (n * n).sum(0)
    inverse = np.where(square > 0.5, 1.0 / np.maximum(square, 1.0), 0.0)
    lam_ref, mu_ref = ref_modulus * lam_hat, ref_modulus * mu_hat
    coupling = (lam_ref + mu_ref) / (mu_ref * (lam_ref + 2.0 * mu_ref))
    out = np.zeros((6, 6) + square.shape)
    for column, (a, b) in enumerate(voigt_pairs):
        traction = np.zeros_like(n)
        traction[a] += n[b]
        if a != b:
            traction[b] += n[a]
        along = (n * traction).sum(0)
        amplitude = inverse * traction / mu_ref - coupling * along * inverse * inverse * n
        for k, (c, d) in enumerate(voigt_pairs):
            out[k, column] = 0.5 * (n[c] * amplitude[d] + n[d] * amplitude[c])
    return out


def effective_green():
    index = np.arange(CELL)
    signed = np.where(index < CELL // 2, index, index - CELL)
    mirror = (-index) % CELL
    half = CELL // 2
    fx, fy = signed[:, None, None], signed[None, :, None]
    given = green_matrix(fx, fy, np.arange(half + 1)[None, None, :])
    turned = given[:, :, mirror][:, :, :, mirror]
    full = np.zeros((6, 6, CELL, CELL, CELL))
    full[..., : half + 1] = given
    for plane in (0, half):
        full[..., plane] = 0.5 * (given[..., plane] + turned[..., plane])
    for plane in range(half + 1, CELL):
        full[..., plane] = turned[..., CELL - plane]
    full[:, 3:] *= 0.5
    return full[:, :, : half + 1].reshape(6, 6, half + 1, PLANE)


def cell_tables():
    green = effective_green()
    coefs = np.zeros((9, 24, PLANE))
    for a in range(6):
        for b in range(a, 6):
            coefs[:, packed[(a, b)]] = green[a, b]
    wide = green.transpose(2, 1, 0, 3).reshape(9, 6, 6 * PLANE)
    upper = wide.astype(bf16).astype(np.float64)
    first = np.zeros((9, 32, 6 * PLANE))
    first[:, 0:6] = upper
    first[:, 6:12] = upper
    first[:, 12:18] = wide - upper
    place = np.arange(PLANE)
    phase = (place // CELL)[:, None] * (place // CELL)[None, :] + (place % CELL)[:, None] * (
        place % CELL
    )[None, :]
    angle = (phase % CELL) * (2.0 * math.pi / CELL)
    cos, sin = np.cos(angle), np.sin(angle)
    forward = np.block([[cos, sin], [-sin, cos]])
    inverse = np.block([[cos, -sin], [sin, cos]]) * (2.0 / VOX)
    return coefs, first, forward, inverse, cos + sin, (cos + sin) / VOX


def parts3(value):
    first = value.astype(bf16)
    rest = value - first.astype(f32)
    second = rest.astype(bf16)
    third = (rest - second.astype(f32)).astype(bf16)
    return jnp.concatenate([first, second, third], axis=0)


def total3(value):
    rows = value.shape[0] // 3
    return value[:rows] + value[rows : 2 * rows] + value[2 * rows :]


def forward_x(v):
    s = [v[x] + v[x + 8] for x in range(8)]
    d = [v[x] - v[x + 8] for x in range(8)]
    a = [s[x] + s[x + 4] for x in range(4)]
    b = [s[x] - s[x + 4] for x in range(4)]
    a02, a13 = a[0] + a[2], a[1] + a[3]
    bm, bp = C2 * (b[1] - b[3]), C2 * (b[1] + b[3])
    p1, p2, p3 = d[1] - d[7], C2 * (d[2] - d[6]), d[3] - d[5]
    q1, q2, q3 = d[1] + d[7], C2 * (d[2] + d[6]), d[3] + d[5]
    re_sum, re_dif = d[0] + p2, d[0] - p2
    re_a, re_b = C1 * p1 + C3 * p3, C3 * p1 - C1 * p3
    im_sum, im_dif = q2 + d[4], q2 - d[4]
    im_a, im_b = C3 * q1 + C1 * q3, C1 * q1 - C3 * q3
    pairs = [
        (re_sum + re_a, im_a + im_sum),
        (b[0] + bm, bp + b[2]),
        (re_dif + re_b, im_b + im_dif),
        (a[0] - a[2], a[1] - a[3]),
        (re_dif - re_b, im_b - im_dif),
        (b[0] - bm, bp - b[2]),
        (re_sum - re_a, im_a - im_sum),
    ]
    return a02 + a13, a02 - a13, pairs


def inverse_x(x0, x8, pairs):
    r = [None] + [pair[0] for pair in pairs]
    m = [None] + [pair[1] for pair in pairs]
    plus, minus = x0 + x8, x0 - x8
    r26p, r26m = r[2] + r[6], C2 * (r[2] - r[6])
    p4 = plus + r[4]
    even = [p4 + r26p, minus + r26m, plus - r[4], minus - r26m, p4 - r26p]
    r17p, r17m, r35p, r35m = r[1] + r[7], r[1] - r[7], r[3] + r[5], r[3] - r[5]
    odd = [r17p + r35p, C1 * r17m + C3 * r35m, C2 * (r17p - r35p), C3 * r17m - C1 * r35m]
    cosine = [None] * 9
    for x in range(4):
        cosine[x] = even[x] + odd[x]
        cosine[8 - x] = even[x] - odd[x]
    cosine[4] = even[4]
    m26p = C2 * (m[2] + m[6])
    s_even = [None, m26p + m[4], m[2] - m[6], m26p - m[4]]
    m17p, m17m, m35p, m35m = m[1] + m[7], m[1] - m[7], m[3] + m[5], m[3] - m[5]
    s_odd = [None, C3 * m17p + C1 * m35p, C2 * (m17m + m35m), C1 * m17p - C3 * m35p]
    sine = [None] * 8
    for x in range(1, 4):
        sine[x] = s_odd[x] + s_even[x]
        sine[8 - x] = s_odd[x] - s_even[x]
    sine[4] = m17m - m35m
    out = [None] * 16
    out[0], out[8] = cosine[0], cosine[8]
    for x in range(1, 8):
        out[x] = cosine[x] + sine[x]
        out[16 - x] = cosine[x] - sine[x]
    return out


def damage_of(e):
    energy = e[0] * e[0] + e[1] * e[1] + e[2] * e[2]
    energy = energy + 2.0 * (e[3] * e[3] + e[4] * e[4] + e[5] * e[5])
    return energy / (energy + kappa_sq)


def unit_law(e, shear):
    volume = lam_hat * (e[0] + e[1] + e[2])
    return [2.0 * mu_hat * e[k] + volume for k in range(3)] + [
        (shear * 2.0 * mu_hat) * e[k] for k in range(3, 6)
    ]


def kernel(
    layers,
    slots,
    count_ref,
    nodes_ref,
    points_ref,
    modulus_hbm,
    pick_hbm,
    strain_hbm,
    damage_hbm,
    voxel_hbm,
    forward_hbm,
    first_hbm,
    inverse_hbm,
    real_forward_hbm,
    real_inverse_hbm,
    coef_hbm,
    force_hbm,
    force_ref,
    new_hbm,
    field,
    spec_c,
    spec_r,
    back_c,
    back_r,
    freq,
    green,
    macro,
    stress_s,
    acc,
    new_ref,
    modulus_ref,
    pick_tab,
    strain_tab,
    damage_ref,
    voxel_ref,
    forward_tab,
    first_tab,
    inverse_tab,
    real_forward,
    real_inverse,
    coef_tab,
    force_tab,
    in_sems,
    out_sems,
):
    sources = (
        modulus_hbm,
        pick_hbm,
        strain_hbm,
        damage_hbm,
        voxel_hbm,
        forward_hbm,
        first_hbm,
        inverse_hbm,
        real_forward_hbm,
        real_inverse_hbm,
        coef_hbm,
        force_hbm,
    )
    targets = (
        modulus_ref,
        pick_tab,
        strain_tab,
        damage_ref,
        voxel_ref,
        forward_tab,
        first_tab,
        inverse_tab,
        real_forward,
        real_inverse,
        coef_tab,
        force_tab,
    )
    loads = [
        pltpu.make_async_copy(source, target, in_sems.at[n])
        for n, (source, target) in enumerate(zip(sources, targets))
    ]
    for load in loads:
        load.start()
    for load in loads[:3]:
        load.wait()
    elems = layers * EXY * EXY
    chunks = slots // ROWS
    count = count_ref[0]

    spread = total3(jnp.dot(parts3(nodes_ref[...]), pick_tab[...], preferred_element_type=f32))
    plane = EXY * EXY
    corners = jnp.concatenate(
        [
            jnp.concatenate(
                [spread[z * 8 : z * 8 + 8, c * plane : (c + 1) * plane] for z in range(layers)],
                axis=1,
            )
            for c in range(4)
        ],
        axis=0,
    )
    strain = jnp.dot(strain_tab[...], corners, precision=HIGHEST, preferred_element_type=f32)
    modulus = modulus_ref[...]
    law = unit_law([strain[k * 8 : k * 8 + 8] for k in range(6)], 1.0)
    stress = jnp.concatenate([modulus * law[k] for k in range(6)], axis=0)
    stress_s[...] = stress

    square = (slots, slots)
    diagonal = lax.broadcasted_iota(jnp.int32, square, 0) == lax.broadcasted_iota(
        jnp.int32, square, 1
    )
    spread_points = jnp.broadcast_to(points_ref[...].astype(f32), square)
    points = jnp.sum(jnp.where(diagonal, spread_points, 0.0), axis=1, keepdims=True)
    points = points.astype(jnp.int32)
    element = points % elems
    gauss = points // elems
    hot = (lax.broadcasted_iota(jnp.int32, (slots, elems), 1) == element).astype(f32).astype(bf16)
    both = parts3(jnp.concatenate([strain, stress], axis=0))
    picked = lax.dot_general(hot, both, (((1,), (1,)), ((), ())), preferred_element_type=f32)
    picked = picked[:, 0:96] + picked[:, 96:192] + picked[:, 192:288]
    lane96 = lax.broadcasted_iota(jnp.int32, (slots, 96), 1)
    own = [
        jnp.sum(jnp.where(lane96 == k * 8 + gauss, picked, 0.0), axis=1, keepdims=True)
        for k in range(12)
    ]
    mean = [own[k].astype(bf16).astype(f32) for k in range(6)]
    for k in range(6):
        macro[k] = jnp.broadcast_to(mean[k], (slots, HALF))

    mean_law = unit_law(mean, 2.0)
    mean_damage = damage_of(mean)
    lane32 = lax.broadcasted_iota(jnp.int32, (slots, 32), 1)
    upper = jnp.zeros((slots, 32), f32)
    for k in range(6):
        high = mean_law[k].astype(bf16).astype(f32)
        upper = jnp.where((lane32 == k) | (lane32 == 12 + k), high, upper)
        upper = jnp.where(lane32 == 6 + k, mean_law[k] - high, upper)
    mean_parts = upper.astype(bf16)
    for load in loads[3:5]:
        load.wait()
    for r in range(chunks):
        rows = slice(r * ROWS, (r + 1) * ROWS)
        for h in range(2):
            lanes = slice(h * HALF, (h + 1) * HALF)
            scalar = []
            for x in range(CELL):
                cols = slice(x * PLANE + h * HALF, x * PLANE + (h + 1) * HALF)
                old = damage_ref[rows, cols].astype(f32)
                young = voxel_ref[rows, cols].astype(f32)
                scalar.append((1.0 - jnp.maximum(old, mean_damage[rows])) * young - ref_modulus)
            x0, x8, pairs = forward_x(scalar)
            spec_r[0, rows, lanes] = x0.astype(bf16)
            spec_r[1, rows, lanes] = x8.astype(bf16)
            for j in range(7):
                spec_c[j, rows, h * HALF : (h + 1) * HALF] = pairs[j][0].astype(bf16)
                spec_c[j, rows, PLANE + h * HALF : PLANE + (h + 1) * HALF] = pairs[j][1].astype(
                    bf16
                )

    def first_c(j, carry):
        spectrum = jnp.dot(spec_c[j, 0:slots], forward_tab[...], preferred_element_type=f32)
        weight = jnp.dot(mean_parts, first_tab[j + 1], preferred_element_type=f32)
        for k in range(6):
            part = weight[:, k * PLANE : (k + 1) * PLANE]
            rows = slice(k * slots, (k + 1) * slots)
            green[rows, 0:PLANE] = (part * spectrum[:, 0:PLANE]).astype(bf16)
            green[rows, PLANE:] = (part * spectrum[:, PLANE:]).astype(bf16)
        back_c[j] = jnp.dot(green[...], inverse_tab[...], preferred_element_type=f32)
        return carry

    def first_r(j, carry):
        spectrum = jnp.dot(spec_r[j, 0:slots], real_forward[...], preferred_element_type=f32)
        weight = jnp.dot(mean_parts, first_tab[j * 8], preferred_element_type=f32)
        for k in range(6):
            part = weight[:, k * PLANE : (k + 1) * PLANE]
            green[k * slots : (k + 1) * slots, 0:PLANE] = (part * spectrum).astype(bf16)
        back_r[j] = jnp.dot(green[:, 0:PLANE], real_inverse[...], preferred_element_type=f32)
        return carry

    def to_strain(k, carry):
        for r in range(chunks):
            rows = pl.ds(pl.multiple_of(k * slots + r * ROWS, ROWS), ROWS)
            base = macro[k, r * ROWS : (r + 1) * ROWS]
            for h in range(2):
                lanes = slice(h * HALF, (h + 1) * HALF)
                upper_lanes = slice(PLANE + h * HALF, PLANE + (h + 1) * HALF)
                pairs = [(back_c[j, rows, lanes], back_c[j, rows, upper_lanes]) for j in range(7)]
                values = inverse_x(back_r[0, rows, lanes], back_r[1, rows, lanes], pairs)
                for x in range(CELL):
                    field[k * CELL + x, r * ROWS : (r + 1) * ROWS, lanes] = base - values[x]
        return carry

    for load in loads[5:]:
        load.wait()
    lax.fori_loop(0, 7, first_c, 0)
    lax.fori_loop(0, 2, first_r, 0)
    lax.fori_loop(0, 6, to_strain, 0)

    def polarize(x, carry):
        cols = pl.ds(pl.multiple_of(x * PLANE, PLANE), PLANE)
        for r in range(chunks):
            rows = slice(r * ROWS, (r + 1) * ROWS)
            e = [field[k * CELL + x, rows] for k in range(6)]
            old = damage_ref[rows, cols].astype(f32)
            young = voxel_ref[rows, cols].astype(f32)
            change = (1.0 - jnp.maximum(old, damage_of(e))) * young - ref_modulus
            for k, unit in enumerate(unit_law(e, 2.0)):
                field[k * CELL + x, rows] = change * unit
        return carry

    def to_spectrum(k, carry):
        for r in range(chunks):
            rows = pl.ds(pl.multiple_of(k * slots + r * ROWS, ROWS), ROWS)
            for h in range(2):
                lanes = slice(h * HALF, (h + 1) * HALF)
                upper_lanes = slice(PLANE + h * HALF, PLANE + (h + 1) * HALF)
                x0, x8, pairs = forward_x(
                    [field[k * CELL + x, r * ROWS : (r + 1) * ROWS, lanes] for x in range(CELL)]
                )
                spec_r[0, rows, lanes] = x0.astype(bf16)
                spec_r[1, rows, lanes] = x8.astype(bf16)
                for j in range(7):
                    spec_c[j, rows, lanes] = pairs[j][0].astype(bf16)
                    spec_c[j, rows, upper_lanes] = pairs[j][1].astype(bf16)
        return carry

    def apply_green(index, planes):
        for h in range(2):
            lanes = slice(h * HALF, (h + 1) * HALF)
            coefs = [
                jnp.broadcast_to(coef_tab[index, c : c + 1, lanes], (ROWS, HALF))
                for c in range(21)
            ]
            for part in range(planes):
                where = slice(part * PLANE + h * HALF, part * PLANE + (h + 1) * HALF)
                for r in range(chunks):
                    t = [
                        freq[k * slots + r * ROWS : k * slots + (r + 1) * ROWS, where]
                        for k in range(6)
                    ]
                    for k in range(6):
                        total = coefs[packed[(k, 0)]] * t[0]
                        for b in range(1, 6):
                            total = total + coefs[packed[(k, b)]] * t[b]
                        green[k * slots + r * ROWS : k * slots + (r + 1) * ROWS, where] = (
                            total.astype(bf16)
                        )

    def second_c(j, carry):
        freq[...] = jnp.dot(spec_c[j], forward_tab[...], preferred_element_type=f32)
        apply_green(j + 1, 2)
        back_c[j] = jnp.dot(green[...], inverse_tab[...], preferred_element_type=f32)
        return carry

    def second_r(j, carry):
        freq[:, 0:PLANE] = jnp.dot(spec_r[j], real_forward[...], preferred_element_type=f32)
        apply_green(j * 8, 1)
        back_r[j] = jnp.dot(green[:, 0:PLANE], real_inverse[...], preferred_element_type=f32)
        return carry

    lax.fori_loop(0, CELL, polarize, 0)
    lax.fori_loop(0, 6, to_spectrum, 0)
    lax.fori_loop(0, 7, second_c, 0)
    lax.fori_loop(0, 2, second_r, 0)
    lax.fori_loop(0, 6, to_strain, 0)

    stores = []
    for r in range(chunks):
        rows = slice(r * ROWS, (r + 1) * ROWS)
        live = lax.broadcasted_iota(jnp.int32, (ROWS, PLANE), 0) + r * ROWS < count

        def finish(x, sums, rows=rows, live=live):
            cols = pl.ds(pl.multiple_of(x * PLANE, PLANE), PLANE)
            e = [field[k * CELL + x, rows] for k in range(6)]
            old = damage_ref[rows, cols].astype(f32)
            young = voxel_ref[rows, cols].astype(f32)
            now = jnp.maximum(old, damage_of(e))
            new_ref[rows, cols] = jnp.where(live, now, old).astype(bf16)
            left = (1.0 - now) * young
            out = []
            for k, unit in enumerate(unit_law(e, 1.0)):
                value = left * unit
                out.append(sums[k] + (value[:, 0:HALF] + value[:, HALF:]))
            return tuple(out)

        sums = lax.fori_loop(0, CELL, finish, (jnp.zeros((ROWS, HALF), f32),) * 6)
        for k in range(6):
            acc[k, rows] = sums[k]
        stores.append(pltpu.make_async_copy(new_ref.at[rows], new_hbm.at[rows], out_sems.at[r]))
        stores[r].start()

    alive = lax.broadcasted_iota(jnp.int32, (slots, 1), 0) < count
    lane128 = lax.broadcasted_iota(jnp.int32, (slots, HALF), 1)
    change = jnp.zeros((slots, HALF), f32)
    for k in range(6):
        cell_mean = jnp.sum(acc[k], axis=1, keepdims=True) * (1.0 / VOX)
        delta = jnp.where(alive, cell_mean.astype(bf16).astype(f32) - own[6 + k], 0.0)
        change = jnp.where(lane128 == k * 8 + gauss, delta, change)
    turned = jnp.transpose(change)[0:48]
    stress = stress_s[...] + total3(jnp.dot(parts3(turned), hot, preferred_element_type=f32))
    contrib = jnp.dot(force_tab[...], stress, precision=HIGHEST, preferred_element_type=f32)
    by_layer = jnp.concatenate(
        [
            jnp.concatenate(
                [contrib[c * 8 : c * 8 + 8, z * plane : (z + 1) * plane] for c in range(4)], axis=1
            )
            for z in range(layers)
        ],
        axis=0,
    )
    force_ref[...] = total3(
        lax.dot_general(
            parts3(by_layer), pick_tab[...], (((1,), (1,)), ((), ())), preferred_element_type=f32
        )
    )
    for store in stores:
        store.wait()


def run_kernel(count, nodes, modulus, points, damage, voxel, layers, interpret=False):
    slots = damage.shape[0]
    to_strain, to_force, pick = macro_tables()
    coefs, first, forward, inverse, real_forward, real_inverse = cell_tables()
    operands = (
        modulus,
        jnp.asarray(pick, bf16),
        jnp.asarray(to_strain, f32),
        damage,
        voxel,
        jnp.asarray(forward, bf16),
        jnp.asarray(first, bf16),
        jnp.asarray(inverse, bf16),
        jnp.asarray(real_forward, bf16),
        jnp.asarray(real_inverse, bf16),
        jnp.asarray(coefs, f32),
        jnp.asarray(to_force, f32),
    )
    vmem, anywhere = pl.BlockSpec(memory_space=pltpu.VMEM), pl.BlockSpec(memory_space=pl.ANY)
    rows = 6 * slots

    def body(*refs):
        kernel(layers, slots, *refs)

    return pl.pallas_call(
        body,
        out_shape=(
            jax.ShapeDtypeStruct((layers * 8, NODE_PAD), f32),
            jax.ShapeDtypeStruct(damage.shape, bf16),
        ),
        in_specs=[pl.BlockSpec(memory_space=pltpu.SMEM), vmem, vmem] + [anywhere] * 12,
        out_specs=(vmem, anywhere),
        scratch_shapes=[
            pltpu.VMEM((6 * CELL, slots, PLANE), f32),
            pltpu.VMEM((7, rows, 2 * PLANE), bf16),
            pltpu.VMEM((2, rows, PLANE), bf16),
            pltpu.VMEM((7, rows, 2 * PLANE), f32),
            pltpu.VMEM((2, rows, PLANE), f32),
            pltpu.VMEM((rows, 2 * PLANE), f32),
            pltpu.VMEM((rows, 2 * PLANE), bf16),
            pltpu.VMEM((6, slots, HALF), f32),
            pltpu.VMEM((48, layers * EXY * EXY), f32),
            pltpu.VMEM((6, slots, HALF), f32),
            pltpu.VMEM(damage.shape, bf16),
        ]
        + [pltpu.VMEM(operand.shape, operand.dtype) for operand in operands]
        + [
            pltpu.SemaphoreType.DMA((len(operands),)),
            pltpu.SemaphoreType.DMA((slots // ROWS,)),
        ],
        compiler_params=pltpu.CompilerParams(vmem_limit_bytes=44 * 1024 * 1024),
        cost_estimate=pl.CostEstimate(flops=10**10, bytes_accessed=8 * 10**6, transcendentals=0),
        interpret=interpret,
    )(count, nodes, points, *operands)


def neighbour(steps, across):
    place = lax.axis_index("dom") * across + lax.axis_index("sub") + steps
    return (place // across, place % across)


def spread_kernel(layers, total, across, moved_ref, nodes_ref, sent, landed, send_sem, recv_sem):
    place = lax.axis_index("dom") * across + lax.axis_index("sub")
    barrier = pltpu.get_barrier_semaphore()

    @pl.when(place > 0)
    def _():
        pl.semaphore_signal(
            barrier, inc=1, device_id=neighbour(-1, across), device_id_type=MESH
        )

    sent[...] = jnp.zeros_like(sent)
    for i in range(3):
        sent[i : i + 1, 0:NODES] = moved_ref[i, layers - 1 : layers, :]
    copy = pltpu.make_async_remote_copy(
        src_ref=sent,
        dst_ref=landed,
        send_sem=send_sem,
        recv_sem=recv_sem,
        device_id=neighbour(1, across),
        device_id_type=MESH,
    )

    @pl.when(place < total - 1)
    def _():
        pl.semaphore_wait(barrier, 1)
        copy.start()

    nodes_ref[...] = jnp.zeros_like(nodes_ref)
    for z in range(layers):
        for cz in range(2):
            for i in range(3):
                if z + cz > 0:
                    row = z * 8 + cz * 3 + i
                    nodes_ref[row : row + 1, 0:NODES] = moved_ref[i, z + cz - 1 : z + cz, :]

    @pl.when(place > 0)
    def _():
        copy.wait_recv()
        nodes_ref[0:3, :] = landed[0:3, :]

    @pl.when(place < total - 1)
    def _():
        copy.wait_send()


def gather_kernel(layers, total, across, force_ref, out_ref, landed, send_sem, recv_sem):
    place = lax.axis_index("dom") * across + lax.axis_index("sub")
    barrier = pltpu.get_barrier_semaphore()

    @pl.when(place < total - 1)
    def _():
        pl.semaphore_signal(
            barrier, inc=1, device_id=neighbour(1, across), device_id_type=MESH
        )

    copy = pltpu.make_async_remote_copy(
        src_ref=force_ref.at[0:8],
        dst_ref=landed,
        send_sem=send_sem,
        recv_sem=recv_sem,
        device_id=neighbour(-1, across),
        device_id_type=MESH,
    )

    @pl.when(place > 0)
    def _():
        pl.semaphore_wait(barrier, 1)
        copy.start()

    for z in range(layers):
        for i in range(3):
            value = force_ref[z * 8 + 3 + i : z * 8 + 4 + i, 0:NODES]
            if z + 1 < layers:
                value = value + force_ref[z * 8 + 8 + i : z * 8 + 9 + i, 0:NODES]
            out_ref[i, z : z + 1, :] = value

    @pl.when(place < total - 1)
    def _():
        copy.wait_recv()
        for i in range(3):
            out_ref[i, layers - 1 : layers, :] += landed[i : i + 1, 0:NODES]

    @pl.when(place > 0)
    def _():
        copy.wait_send()


def exchange(function, value, shape, scratch, collective_id):
    vmem = pl.BlockSpec(memory_space=pltpu.VMEM)
    tile = pltpu.VMEM((8, NODE_PAD), f32)
    return pl.pallas_call(
        function,
        out_shape=jax.ShapeDtypeStruct(shape, f32),
        in_specs=[vmem],
        out_specs=vmem,
        scratch_shapes=[tile] * scratch + [pltpu.SemaphoreType.DMA] * 2,
        compiler_params=pltpu.CompilerParams(collective_id=collective_id, has_side_effects=True),
    )(value)


def body(displacement, macro_modulus, damaged_count, damaged_points, damage, voxel_modulus):
    layers = displacement.shape[1]
    across = lax.axis_size("sub")
    total = lax.axis_size("dom") * across
    nodes = exchange(
        functools.partial(spread_kernel, layers, total, across),
        displacement,
        (layers * 8, NODE_PAD),
        2,
        0,
    )
    force, new_damage = run_kernel(
        damaged_count, nodes, macro_modulus, damaged_points, damage, voxel_modulus, layers
    )
    own_forces = exchange(
        functools.partial(gather_kernel, layers, total, across), force, displacement.shape, 1, 1
    )
    return (own_forces, new_damage)


def solution(mesh):
    return jax.shard_map(
        body,
        mesh=mesh,
        in_specs=(
            P(None, ("dom", "sub"), None),
            P(None, ("dom", "sub")),
            P(("dom", "sub")),
            P(("dom", "sub"), None),
            P(("dom", "sub"), None),
            P(("dom", "sub"), None),
        ),
        out_specs=(P(None, ("dom", "sub"), None), P(("dom", "sub"), None)),
        check_vma=False,
    )
```

```python
import functools
import math

import jax
import jax.numpy as jnp
import numpy as np
from jax import lax
from jax.experimental import pallas as pl
from jax.experimental.pallas import tpu as pltpu
from jax.sharding import PartitionSpec as P

CELL = 16
PLANE = CELL * CELL
VOX = CELL**3
EXY = 16
NODES = (EXY + 1) ** 2
NODE_PAD = 384
HALF = 128
ROWS = 16

lam_hat = 0.2 / 0.72
mu_hat = 1.0 / 2.4
ref_modulus = 2.0
kappa_sq = 4.0
voigt_pairs = ((0, 0), (1, 1), (2, 2), (1, 2), (0, 2), (0, 1))
packed = {}
for _a in range(6):
    for _b in range(_a, 6):
        packed[(_a, _b)] = packed[(_b, _a)] = len(packed) - sum(
            1 for _p in packed if _p[0] > _p[1]
        )
C1, C2, C3 = (math.cos(math.pi * n / 8) for n in (1, 2, 3))
f32, bf16 = jnp.float32, jnp.bfloat16
MESH = pl.DeviceIdType.MESH
HIGHEST = lax.Precision.HIGHEST


def shape_table():
    gauss_coord = 1.0 / math.sqrt(3.0)
    gradients = np.zeros((8, 8, 3))
    for corner in range(8):
        signs = [2 * (corner >> d & 1) - 1 for d in range(3)]
        for gauss_no in range(8):
            coords = [(2 * (gauss_no >> d & 1) - 1) * gauss_coord for d in range(3)]
            factor = [(1.0 + signs[d] * coords[d]) / 2.0 for d in range(3)]
            for d in range(3):
                value = float(signs[d])
                for other in range(3):
                    if other != d:
                        value *= factor[other]
                gradients[corner, gauss_no, d] = value
    return gradients


def macro_tables():
    table = shape_table()
    to_strain = np.zeros((48, 32))
    to_force = np.zeros((32, 48))
    for corner in range(8):
        base = (corner & 3) * 8 + (corner >> 2) * 3
        for k, (a, b) in enumerate(voigt_pairs):
            for q in range(8):
                to_strain[k * 8 + q, base + a] += 0.5 * table[corner, q, b]
                to_strain[k * 8 + q, base + b] += 0.5 * table[corner, q, a]
                to_force[base + a, k * 8 + q] += 0.125 * table[corner, q, b]
                if a != b:
                    to_force[base + b, k * 8 + q] += 0.125 * table[corner, q, a]
    pick = np.zeros((NODE_PAD, 4 * EXY * EXY))
    for cy in range(2):
        for cx in range(2):
            for y in range(EXY):
                for x in range(EXY):
                    column = (2 * cy + cx) * EXY * EXY + y * EXY + x
                    pick[(y + cy) * (EXY + 1) + x + cx, column] = 1.0
    return to_strain, to_force, pick


def green_matrix(nx, ny, nz):
    n = np.stack(np.broadcast_arrays(nx, ny, nz)).astype(np.float64)
    square = (n * n).sum(0)
    inverse = np.where(square > 0.5, 1.0 / np.maximum(square, 1.0), 0.0)
    lam_ref, mu_ref = ref_modulus * lam_hat, ref_modulus * mu_hat
    coupling = (lam_ref + mu_ref) / (mu_ref * (lam_ref + 2.0 * mu_ref))
    out = np.zeros((6, 6) + square.shape)
    for column, (a, b) in enumerate(voigt_pairs):
        traction = np.zeros_like(n)
        traction[a] += n[b]
        if a != b:
            traction[b] += n[a]
        along = (n * traction).sum(0)
        amplitude = inverse * traction / mu_ref - coupling * along * inverse * inverse * n
        for k, (c, d) in enumerate(voigt_pairs):
            out[k, column] = 0.5 * (n[c] * amplitude[d] + n[d] * amplitude[c])
    return out


def effective_green():
    index = np.arange(CELL)
    signed = np.where(index < CELL // 2, index, index - CELL)
    mirror = (-index) % CELL
    half = CELL // 2
    fx, fy = signed[:, None, None], signed[None, :, None]
    given = green_matrix(fx, fy, np.arange(half + 1)[None, None, :])
    turned = given[:, :, mirror][:, :, :, mirror]
    full = np.zeros((6, 6, CELL, CELL, CELL))
    full[..., : half + 1] = given
    for plane in (0, half):
        full[..., plane] = 0.5 * (given[..., plane] + turned[..., plane])
    for plane in range(half + 1, CELL):
        full[..., plane] = turned[..., CELL - plane]
    full[:, 3:] *= 0.5
    return full[:, :, : half + 1].reshape(6, 6, half + 1, PLANE)


def cell_tables():
    green = effective_green()
    coefs = np.zeros((9, 24, PLANE))
    for a in range(6):
        for b in range(a, 6):
            coefs[:, packed[(a, b)]] = green[a, b]
    wide = green.transpose(2, 1, 0, 3).reshape(9, 6, 6 * PLANE)
    upper = wide.astype(bf16).astype(np.float64)
    first = np.zeros((9, 32, 6 * PLANE))
    first[:, 0:6] = upper
    first[:, 6:12] = upper
    first[:, 12:18] = wide - upper
    place = np.arange(PLANE)
    phase = (place // CELL)[:, None] * (place // CELL)[None, :] + (place % CELL)[:, None] * (
        place % CELL
    )[None, :]
    angle = (phase % CELL) * (2.0 * math.pi / CELL)
    cos, sin = np.cos(angle), np.sin(angle)
    forward = np.block([[cos, sin], [-sin, cos]])
    inverse = np.block([[cos, -sin], [sin, cos]]) * (2.0 / VOX)
    return coefs, first, forward, inverse, cos + sin, (cos + sin) / VOX


def parts3(value):
    first = value.astype(bf16)
    rest = value - first.astype(f32)
    second = rest.astype(bf16)
    third = (rest - second.astype(f32)).astype(bf16)
    return jnp.concatenate([first, second, third], axis=0)


def total3(value):
    rows = value.shape[0] // 3
    return value[:rows] + value[rows : 2 * rows] + value[2 * rows :]


def forward_x(v):
    s = [v[x] + v[x + 8] for x in range(8)]
    d = [v[x] - v[x + 8] for x in range(8)]
    a = [s[x] + s[x + 4] for x in range(4)]
    b = [s[x] - s[x + 4] for x in range(4)]
    a02, a13 = a[0] + a[2], a[1] + a[3]
    bm, bp = C2 * (b[1] - b[3]), C2 * (b[1] + b[3])
    p1, p2, p3 = d[1] - d[7], C2 * (d[2] - d[6]), d[3] - d[5]
    q1, q2, q3 = d[1] + d[7], C2 * (d[2] + d[6]), d[3] + d[5]
    re_sum, re_dif = d[0] + p2, d[0] - p2
    re_a, re_b = C1 * p1 + C3 * p3, C3 * p1 - C1 * p3
    im_sum, im_dif = q2 + d[4], q2 - d[4]
    im_a, im_b = C3 * q1 + C1 * q3, C1 * q1 - C3 * q3
    pairs = [
        (re_sum + re_a, im_a + im_sum),
        (b[0] + bm, bp + b[2]),
        (re_dif + re_b, im_b + im_dif),
        (a[0] - a[2], a[1] - a[3]),
        (re_dif - re_b, im_b - im_dif),
        (b[0] - bm, bp - b[2]),
        (re_sum - re_a, im_a - im_sum),
    ]
    return a02 + a13, a02 - a13, pairs


def inverse_x(x0, x8, pairs):
    r = [None] + [pair[0] for pair in pairs]
    m = [None] + [pair[1] for pair in pairs]
    plus, minus = x0 + x8, x0 - x8
    r26p, r26m = r[2] + r[6], C2 * (r[2] - r[6])
    p4 = plus + r[4]
    even = [p4 + r26p, minus + r26m, plus - r[4], minus - r26m, p4 - r26p]
    r17p, r17m, r35p, r35m = r[1] + r[7], r[1] - r[7], r[3] + r[5], r[3] - r[5]
    odd = [r17p + r35p, C1 * r17m + C3 * r35m, C2 * (r17p - r35p), C3 * r17m - C1 * r35m]
    cosine = [None] * 9
    for x in range(4):
        cosine[x] = even[x] + odd[x]
        cosine[8 - x] = even[x] - odd[x]
    cosine[4] = even[4]
    m26p = C2 * (m[2] + m[6])
    s_even = [None, m26p + m[4], m[2] - m[6], m26p - m[4]]
    m17p, m17m, m35p, m35m = m[1] + m[7], m[1] - m[7], m[3] + m[5], m[3] - m[5]
    s_odd = [None, C3 * m17p + C1 * m35p, C2 * (m17m + m35m), C1 * m17p - C3 * m35p]
    sine = [None] * 8
    for x in range(1, 4):
        sine[x] = s_odd[x] + s_even[x]
        sine[8 - x] = s_odd[x] - s_even[x]
    sine[4] = m17m - m35m
    out = [None] * 16
    out[0], out[8] = cosine[0], cosine[8]
    for x in range(1, 8):
        out[x] = cosine[x] + sine[x]
        out[16 - x] = cosine[x] - sine[x]
    return out


def damage_of(e):
    energy = e[0] * e[0] + e[1] * e[1] + e[2] * e[2]
    energy = energy + 2.0 * (e[3] * e[3] + e[4] * e[4] + e[5] * e[5])
    return energy / (energy + kappa_sq)


def unit_law(e, shear):
    volume = lam_hat * (e[0] + e[1] + e[2])
    return [2.0 * mu_hat * e[k] + volume for k in range(3)] + [
        (shear * 2.0 * mu_hat) * e[k] for k in range(3, 6)
    ]


def neighbour(steps, across):
    place = lax.axis_index("dom") * across + lax.axis_index("sub") + steps
    return (place // across, place % across)


def kernel(
    layers,
    slots,
    total,
    across,
    count_ref,
    moved_hbm,
    points_hbm,
    modulus_hbm,
    pick_hbm,
    strain_hbm,
    damage_hbm,
    voxel_hbm,
    forward_hbm,
    first_hbm,
    inverse_hbm,
    real_forward_hbm,
    real_inverse_hbm,
    coef_hbm,
    force_hbm,
    force_ref,
    new_hbm,
    field,
    spec_c,
    spec_r,
    back_c,
    back_r,
    freq,
    green,
    macro,
    stress_s,
    acc,
    new_ref,
    nodes_ref,
    forces,
    sent,
    landed_up,
    landed_down,
    moved_ref,
    points_ref,
    modulus_ref,
    pick_tab,
    strain_tab,
    damage_ref,
    voxel_ref,
    forward_tab,
    first_tab,
    inverse_tab,
    real_forward,
    real_inverse,
    coef_tab,
    force_tab,
    in_sems,
    out_sems,
    send_sems,
    recv_sems,
):
    place = lax.axis_index("dom") * across + lax.axis_index("sub")
    barrier = pltpu.get_barrier_semaphore()
    has_below, has_above = place > 0, place < total - 1

    @pl.when(has_below)
    def _():
        pl.semaphore_signal(barrier, inc=1, device_id=neighbour(-1, across), device_id_type=MESH)

    @pl.when(has_above)
    def _():
        pl.semaphore_signal(barrier, inc=1, device_id=neighbour(1, across), device_id_type=MESH)

    sources = (
        moved_hbm,
        points_hbm,
        modulus_hbm,
        pick_hbm,
        strain_hbm,
        damage_hbm,
        voxel_hbm,
        forward_hbm,
        first_hbm,
        inverse_hbm,
        real_forward_hbm,
        real_inverse_hbm,
        coef_hbm,
        force_hbm,
    )
    targets = (
        moved_ref,
        points_ref,
        modulus_ref,
        pick_tab,
        strain_tab,
        damage_ref,
        voxel_ref,
        forward_tab,
        first_tab,
        inverse_tab,
        real_forward,
        real_inverse,
        coef_tab,
        force_tab,
    )
    loads = [
        pltpu.make_async_copy(source, target, in_sems.at[n])
        for n, (source, target) in enumerate(zip(sources, targets))
    ]
    for load in loads:
        load.start()

    loads[0].wait()
    sent[...] = jnp.zeros_like(sent)
    for i in range(3):
        sent[i : i + 1, 0:NODES] = moved_ref[i, layers - 1 : layers, :]
    upward = pltpu.make_async_remote_copy(
        src_ref=sent,
        dst_ref=landed_up,
        send_sem=send_sems.at[0],
        recv_sem=recv_sems.at[0],
        device_id=neighbour(1, across),
        device_id_type=MESH,
    )

    pl.semaphore_wait(barrier, jnp.minimum(place, 1) + jnp.minimum(total - 1 - place, 1))

    @pl.when(has_above)
    def _():
        upward.start()

    nodes_ref[...] = jnp.zeros_like(nodes_ref)
    for z in range(layers):
        for cz in range(2):
            for i in range(3):
                if z + cz > 0:
                    row = z * 8 + cz * 3 + i
                    nodes_ref[row : row + 1, 0:NODES] = moved_ref[i, z + cz - 1 : z + cz, :]
    for load in loads[1:5]:
        load.wait()

    @pl.when(has_below)
    def _():
        upward.wait_recv()
        nodes_ref[0:3, :] = landed_up[0:3, :]

    elems = layers * EXY * EXY
    chunks = slots // ROWS
    count = count_ref[0]

    spread = total3(jnp.dot(parts3(nodes_ref[...]), pick_tab[...], preferred_element_type=f32))
    plane = EXY * EXY
    corners = jnp.concatenate(
        [
            jnp.concatenate(
                [spread[z * 8 : z * 8 + 8, c * plane : (c + 1) * plane] for z in range(layers)],
                axis=1,
            )
            for c in range(4)
        ],
        axis=0,
    )
    strain = jnp.dot(strain_tab[...], corners, precision=HIGHEST, preferred_element_type=f32)
    modulus = modulus_ref[...]
    law = unit_law([strain[k * 8 : k * 8 + 8] for k in range(6)], 1.0)
    stress = jnp.concatenate([modulus * law[k] for k in range(6)], axis=0)
    stress_s[...] = stress

    square = (slots, slots)
    diagonal = lax.broadcasted_iota(jnp.int32, square, 0) == lax.broadcasted_iota(
        jnp.int32, square, 1
    )
    spread_points = jnp.broadcast_to(points_ref[...].astype(f32), square)
    points = jnp.sum(jnp.where(diagonal, spread_points, 0.0), axis=1, keepdims=True)
    points = points.astype(jnp.int32)
    element = points % elems
    gauss = points // elems
    hot = (lax.broadcasted_iota(jnp.int32, (slots, elems), 1) == element).astype(f32).astype(bf16)
    both = parts3(jnp.concatenate([strain, stress], axis=0))
    picked = lax.dot_general(hot, both, (((1,), (1,)), ((), ())), preferred_element_type=f32)
    picked = picked[:, 0:96] + picked[:, 96:192] + picked[:, 192:288]
    lane96 = lax.broadcasted_iota(jnp.int32, (slots, 96), 1)
    own = [
        jnp.sum(jnp.where(lane96 == k * 8 + gauss, picked, 0.0), axis=1, keepdims=True)
        for k in range(12)
    ]
    mean = [own[k].astype(bf16).astype(f32) for k in range(6)]
    for k in range(6):
        macro[k] = jnp.broadcast_to(mean[k], (slots, HALF))

    mean_law = unit_law(mean, 2.0)
    mean_damage = damage_of(mean)
    lane32 = lax.broadcasted_iota(jnp.int32, (slots, 32), 1)
    upper = jnp.zeros((slots, 32), f32)
    for k in range(6):
        high = mean_law[k].astype(bf16).astype(f32)
        upper = jnp.where((lane32 == k) | (lane32 == 12 + k), high, upper)
        upper = jnp.where(lane32 == 6 + k, mean_law[k] - high, upper)
    mean_parts = upper.astype(bf16)
    for load in loads[5:7]:
        load.wait()
    for r in range(chunks):
        rows = slice(r * ROWS, (r + 1) * ROWS)
        for h in range(2):
            lanes = slice(h * HALF, (h + 1) * HALF)
            scalar = []
            for x in range(CELL):
                cols = slice(x * PLANE + h * HALF, x * PLANE + (h + 1) * HALF)
                old = damage_ref[rows, cols].astype(f32)
                young = voxel_ref[rows, cols].astype(f32)
                scalar.append((1.0 - jnp.maximum(old, mean_damage[rows])) * young - ref_modulus)
            x0, x8, pairs = forward_x(scalar)
            spec_r[0, rows, lanes] = x0.astype(bf16)
            spec_r[1, rows, lanes] = x8.astype(bf16)
            for j in range(7):
                spec_c[j, rows, h * HALF : (h + 1) * HALF] = pairs[j][0].astype(bf16)
                spec_c[j, rows, PLANE + h * HALF : PLANE + (h + 1) * HALF] = pairs[j][1].astype(
                    bf16
                )

    def first_c(j, carry):
        spectrum = jnp.dot(spec_c[j, 0:slots], forward_tab[...], preferred_element_type=f32)
        weight = jnp.dot(mean_parts, first_tab[j + 1], preferred_element_type=f32)
        for k in range(6):
            part = weight[:, k * PLANE : (k + 1) * PLANE]
            rows = slice(k * slots, (k + 1) * slots)
            green[rows, 0:PLANE] = (part * spectrum[:, 0:PLANE]).astype(bf16)
            green[rows, PLANE:] = (part * spectrum[:, PLANE:]).astype(bf16)
        back_c[j] = jnp.dot(green[...], inverse_tab[...], preferred_element_type=f32)
        return carry

    def first_r(j, carry):
        spectrum = jnp.dot(spec_r[j, 0:slots], real_forward[...], preferred_element_type=f32)
        weight = jnp.dot(mean_parts, first_tab[j * 8], preferred_element_type=f32)
        for k in range(6):
            part = weight[:, k * PLANE : (k + 1) * PLANE]
            green[k * slots : (k + 1) * slots, 0:PLANE] = (part * spectrum).astype(bf16)
        back_r[j] = jnp.dot(green[:, 0:PLANE], real_inverse[...], preferred_element_type=f32)
        return carry

    def to_strain(k, carry):
        for r in range(chunks):
            rows = pl.ds(pl.multiple_of(k * slots + r * ROWS, ROWS), ROWS)
            base = macro[k, r * ROWS : (r + 1) * ROWS]
            for h in range(2):
                lanes = slice(h * HALF, (h + 1) * HALF)
                upper_lanes = slice(PLANE + h * HALF, PLANE + (h + 1) * HALF)
                pairs = [(back_c[j, rows, lanes], back_c[j, rows, upper_lanes]) for j in range(7)]
                values = inverse_x(back_r[0, rows, lanes], back_r[1, rows, lanes], pairs)
                for x in range(CELL):
                    field[k * CELL + x, r * ROWS : (r + 1) * ROWS, lanes] = base - values[x]
        return carry

    for load in loads[7:]:
        load.wait()
    lax.fori_loop(0, 7, first_c, 0)
    lax.fori_loop(0, 2, first_r, 0)
    lax.fori_loop(0, 6, to_strain, 0)

    def polarize(x, carry):
        cols = pl.ds(pl.multiple_of(x * PLANE, PLANE), PLANE)
        for r in range(chunks):
            rows = slice(r * ROWS, (r + 1) * ROWS)
            e = [field[k * CELL + x, rows] for k in range(6)]
            old = damage_ref[rows, cols].astype(f32)
            young = voxel_ref[rows, cols].astype(f32)
            change = (1.0 - jnp.maximum(old, damage_of(e))) * young - ref_modulus
            for k, unit in enumerate(unit_law(e, 2.0)):
                field[k * CELL + x, rows] = change * unit
        return carry

    def to_spectrum(k, carry):
        for r in range(chunks):
            rows = pl.ds(pl.multiple_of(k * slots + r * ROWS, ROWS), ROWS)
            for h in range(2):
                lanes = slice(h * HALF, (h + 1) * HALF)
                upper_lanes = slice(PLANE + h * HALF, PLANE + (h + 1) * HALF)
                x0, x8, pairs = forward_x(
                    [field[k * CELL + x, r * ROWS : (r + 1) * ROWS, lanes] for x in range(CELL)]
                )
                spec_r[0, rows, lanes] = x0.astype(bf16)
                spec_r[1, rows, lanes] = x8.astype(bf16)
                for j in range(7):
                    spec_c[j, rows, lanes] = pairs[j][0].astype(bf16)
                    spec_c[j, rows, upper_lanes] = pairs[j][1].astype(bf16)
        return carry

    def apply_green(index, planes):
        for h in range(2):
            lanes = slice(h * HALF, (h + 1) * HALF)
            coefs = [
                jnp.broadcast_to(coef_tab[index, c : c + 1, lanes], (ROWS, HALF))
                for c in range(21)
            ]
            for part in range(planes):
                where = slice(part * PLANE + h * HALF, part * PLANE + (h + 1) * HALF)
                for r in range(chunks):
                    t = [
                        freq[k * slots + r * ROWS : k * slots + (r + 1) * ROWS, where]
                        for k in range(6)
                    ]
                    for k in range(6):
                        total = coefs[packed[(k, 0)]] * t[0]
                        for b in range(1, 6):
                            total = total + coefs[packed[(k, b)]] * t[b]
                        green[k * slots + r * ROWS : k * slots + (r + 1) * ROWS, where] = (
                            total.astype(bf16)
                        )

    def second_c(j, carry):
        freq[...] = jnp.dot(spec_c[j], forward_tab[...], preferred_element_type=f32)
        apply_green(j + 1, 2)
        back_c[j] = jnp.dot(green[...], inverse_tab[...], preferred_element_type=f32)
        return carry

    def second_r(j, carry):
        freq[:, 0:PLANE] = jnp.dot(spec_r[j], real_forward[...], preferred_element_type=f32)
        apply_green(j * 8, 1)
        back_r[j] = jnp.dot(green[:, 0:PLANE], real_inverse[...], preferred_element_type=f32)
        return carry

    lax.fori_loop(0, CELL, polarize, 0)
    lax.fori_loop(0, 6, to_spectrum, 0)
    lax.fori_loop(0, 7, second_c, 0)
    lax.fori_loop(0, 2, second_r, 0)
    lax.fori_loop(0, 6, to_strain, 0)

    stores = []
    for r in range(chunks):
        rows = slice(r * ROWS, (r + 1) * ROWS)
        live = lax.broadcasted_iota(jnp.int32, (ROWS, PLANE), 0) + r * ROWS < count

        def finish(x, sums, rows=rows, live=live):
            cols = pl.ds(pl.multiple_of(x * PLANE, PLANE), PLANE)
            e = [field[k * CELL + x, rows] for k in range(6)]
            old = damage_ref[rows, cols].astype(f32)
            young = voxel_ref[rows, cols].astype(f32)
            now = jnp.maximum(old, damage_of(e))
            new_ref[rows, cols] = jnp.where(live, now, old).astype(bf16)
            left = (1.0 - now) * young
            out = []
            for k, unit in enumerate(unit_law(e, 1.0)):
                value = left * unit
                out.append(sums[k] + (value[:, 0:HALF] + value[:, HALF:]))
            return tuple(out)

        sums = lax.fori_loop(0, CELL, finish, (jnp.zeros((ROWS, HALF), f32),) * 6)
        for k in range(6):
            acc[k, rows] = sums[k]
        stores.append(pltpu.make_async_copy(new_ref.at[rows], new_hbm.at[rows], out_sems.at[r]))
        stores[r].start()

    alive = lax.broadcasted_iota(jnp.int32, (slots, 1), 0) < count
    lane128 = lax.broadcasted_iota(jnp.int32, (slots, HALF), 1)
    change = jnp.zeros((slots, HALF), f32)
    for k in range(6):
        cell_mean = jnp.sum(acc[k], axis=1, keepdims=True) * (1.0 / VOX)
        delta = jnp.where(alive, cell_mean.astype(bf16).astype(f32) - own[6 + k], 0.0)
        change = jnp.where(lane128 == k * 8 + gauss, delta, change)
    turned = jnp.transpose(change)[0:48]
    stress = stress_s[...] + total3(jnp.dot(parts3(turned), hot, preferred_element_type=f32))
    contrib = jnp.dot(force_tab[...], stress, precision=HIGHEST, preferred_element_type=f32)
    by_layer = jnp.concatenate(
        [
            jnp.concatenate(
                [contrib[c * 8 : c * 8 + 8, z * plane : (z + 1) * plane] for c in range(4)], axis=1
            )
            for z in range(layers)
        ],
        axis=0,
    )
    forces[...] = total3(
        lax.dot_general(
            parts3(by_layer), pick_tab[...], (((1,), (1,)), ((), ())), preferred_element_type=f32
        )
    )

    downward = pltpu.make_async_remote_copy(
        src_ref=forces.at[0:8],
        dst_ref=landed_down,
        send_sem=send_sems.at[1],
        recv_sem=recv_sems.at[1],
        device_id=neighbour(-1, across),
        device_id_type=MESH,
    )

    @pl.when(has_below)
    def _():
        downward.start()

    force_ref[...] = jnp.zeros_like(force_ref)
    for z in range(layers):
        for i in range(3):
            value = forces[z * 8 + 3 + i : z * 8 + 4 + i, :]
            if z + 1 < layers:
                value = value + forces[z * 8 + 8 + i : z * 8 + 9 + i, :]
            force_ref[i * layers + z : i * layers + z + 1, :] = value
    for store in stores:
        store.wait()

    @pl.when(has_above)
    def _():
        downward.wait_recv()
        for i in range(3):
            row = i * layers + layers - 1
            force_ref[row : row + 1, :] = force_ref[row : row + 1, :] + landed_down[i : i + 1, :]
        upward.wait_send()

    @pl.when(has_below)
    def _():
        downward.wait_send()


def run_kernel(count, moved, modulus, points, damage, voxel, line):
    slots = damage.shape[0]
    layers = moved.shape[1]
    to_strain, to_force, pick = macro_tables()
    coefs, first, forward, inverse, real_forward, real_inverse = cell_tables()
    operands = (
        moved,
        points,
        modulus,
        jnp.asarray(pick, bf16),
        jnp.asarray(to_strain, f32),
        damage,
        voxel,
        jnp.asarray(forward, bf16),
        jnp.asarray(first, bf16),
        jnp.asarray(inverse, bf16),
        jnp.asarray(real_forward, bf16),
        jnp.asarray(real_inverse, bf16),
        jnp.asarray(coefs, f32),
        jnp.asarray(to_force, f32),
    )
    vmem, hbm = pl.BlockSpec(memory_space=pltpu.VMEM), pl.BlockSpec(memory_space=pltpu.HBM)
    rows = 6 * slots

    def body(*refs):
        kernel(layers, slots, *line, *refs)

    return pl.pallas_call(
        body,
        out_shape=(
            jax.ShapeDtypeStruct((layers * 4, NODE_PAD), f32),
            jax.ShapeDtypeStruct(damage.shape, bf16),
        ),
        in_specs=[pl.BlockSpec(memory_space=pltpu.SMEM)] + [hbm] * len(operands),
        out_specs=(vmem, hbm),
        scratch_shapes=[
            pltpu.VMEM((6 * CELL, slots, PLANE), f32),
            pltpu.VMEM((7, rows, 2 * PLANE), bf16),
            pltpu.VMEM((2, rows, PLANE), bf16),
            pltpu.VMEM((7, rows, 2 * PLANE), f32),
            pltpu.VMEM((2, rows, PLANE), f32),
            pltpu.VMEM((rows, 2 * PLANE), f32),
            pltpu.VMEM((rows, 2 * PLANE), bf16),
            pltpu.VMEM((6, slots, HALF), f32),
            pltpu.VMEM((48, layers * EXY * EXY), f32),
            pltpu.VMEM((6, slots, HALF), f32),
            pltpu.VMEM(damage.shape, bf16),
            pltpu.VMEM((layers * 8, NODE_PAD), f32),
            pltpu.VMEM((layers * 8, NODE_PAD), f32),
        ]
        + [pltpu.VMEM((8, NODE_PAD), f32)] * 3
        + [pltpu.VMEM(operand.shape, operand.dtype) for operand in operands]
        + [
            pltpu.SemaphoreType.DMA((len(operands),)),
            pltpu.SemaphoreType.DMA((slots // ROWS,)),
            pltpu.SemaphoreType.DMA((2,)),
            pltpu.SemaphoreType.DMA((2,)),
        ],
        compiler_params=pltpu.CompilerParams(
            vmem_limit_bytes=44 * 1024 * 1024, collective_id=0, has_side_effects=True
        ),
        cost_estimate=pl.CostEstimate(flops=10**10, bytes_accessed=8 * 10**6, transcendentals=0),
    )(count, *operands)


def body(displacement, macro_modulus, damaged_count, damaged_points, damage, voxel_modulus):
    layers = displacement.shape[1]
    across = lax.axis_size("sub")
    total = lax.axis_size("dom") * across
    force, new_damage = run_kernel(
        damaged_count,
        displacement,
        macro_modulus,
        damaged_points,
        damage,
        voxel_modulus,
        (total, across),
    )
    return (force[: 3 * layers].reshape(3, layers, NODE_PAD)[:, :, :NODES], new_damage)


def solution(mesh):
    return jax.shard_map(
        body,
        mesh=mesh,
        in_specs=(
            P(None, ("dom", "sub"), None),
            P(None, ("dom", "sub")),
            P(("dom", "sub")),
            P(("dom", "sub"), None),
            P(("dom", "sub"), None),
            P(("dom", "sub"), None),
        ),
        out_specs=(P(None, ("dom", "sub"), None), P(("dom", "sub"), None)),
        check_vma=False,
    )
```

```python
import functools
import math

import jax
import jax.numpy as jnp
import numpy as np
from jax import lax
from jax.experimental import pallas as pl
from jax.experimental.pallas import tpu as pltpu
from jax.sharding import PartitionSpec as P

CELL = 16
PLANE = CELL * CELL
VOX = CELL**3
EXY = 16
NODES = (EXY + 1) ** 2
NODE_PAD = 384
HALF = 128
ROWS = 16

lam_hat = 0.2 / 0.72
mu_hat = 1.0 / 2.4
ref_modulus = 2.0
kappa_sq = 4.0
voigt_pairs = ((0, 0), (1, 1), (2, 2), (1, 2), (0, 2), (0, 1))
packed = {}
for _a in range(6):
    for _b in range(_a, 6):
        packed[(_a, _b)] = packed[(_b, _a)] = len(packed) - sum(
            1 for _p in packed if _p[0] > _p[1]
        )
C1, C2, C3 = (math.cos(math.pi * n / 8) for n in (1, 2, 3))
f32, bf16 = jnp.float32, jnp.bfloat16
MESH = pl.DeviceIdType.MESH
HIGHEST = lax.Precision.HIGHEST


def shape_table():
    gauss_coord = 1.0 / math.sqrt(3.0)
    gradients = np.zeros((8, 8, 3))
    for corner in range(8):
        signs = [2 * (corner >> d & 1) - 1 for d in range(3)]
        for gauss_no in range(8):
            coords = [(2 * (gauss_no >> d & 1) - 1) * gauss_coord for d in range(3)]
            factor = [(1.0 + signs[d] * coords[d]) / 2.0 for d in range(3)]
            for d in range(3):
                value = float(signs[d])
                for other in range(3):
                    if other != d:
                        value *= factor[other]
                gradients[corner, gauss_no, d] = value
    return gradients


def macro_tables():
    table = shape_table()
    to_strain = np.zeros((48, 32))
    to_force = np.zeros((32, 48))
    for corner in range(8):
        base = (corner & 3) * 8 + (corner >> 2) * 3
        for k, (a, b) in enumerate(voigt_pairs):
            for q in range(8):
                to_strain[k * 8 + q, base + a] += 0.5 * table[corner, q, b]
                to_strain[k * 8 + q, base + b] += 0.5 * table[corner, q, a]
                to_force[base + a, k * 8 + q] += 0.125 * table[corner, q, b]
                if a != b:
                    to_force[base + b, k * 8 + q] += 0.125 * table[corner, q, a]
    pick = np.zeros((NODE_PAD, 4 * EXY * EXY))
    for cy in range(2):
        for cx in range(2):
            for y in range(EXY):
                for x in range(EXY):
                    column = (2 * cy + cx) * EXY * EXY + y * EXY + x
                    pick[(y + cy) * (EXY + 1) + x + cx, column] = 1.0
    return to_strain, to_force, pick


def green_matrix(nx, ny, nz):
    n = np.stack(np.broadcast_arrays(nx, ny, nz)).astype(np.float64)
    square = (n * n).sum(0)
    inverse = np.where(square > 0.5, 1.0 / np.maximum(square, 1.0), 0.0)
    lam_ref, mu_ref = ref_modulus * lam_hat, ref_modulus * mu_hat
    coupling = (lam_ref + mu_ref) / (mu_ref * (lam_ref + 2.0 * mu_ref))
    out = np.zeros((6, 6) + square.shape)
    for column, (a, b) in enumerate(voigt_pairs):
        traction = np.zeros_like(n)
        traction[a] += n[b]
        if a != b:
            traction[b] += n[a]
        along = (n * traction).sum(0)
        amplitude = inverse * traction / mu_ref - coupling * along * inverse * inverse * n
        for k, (c, d) in enumerate(voigt_pairs):
            out[k, column] = 0.5 * (n[c] * amplitude[d] + n[d] * amplitude[c])
    return out


def effective_green():
    index = np.arange(CELL)
    signed = np.where(index < CELL // 2, index, index - CELL)
    mirror = (-index) % CELL
    half = CELL // 2
    fx, fy = signed[:, None, None], signed[None, :, None]
    given = green_matrix(fx, fy, np.arange(half + 1)[None, None, :])
    turned = given[:, :, mirror][:, :, :, mirror]
    full = np.zeros((6, 6, CELL, CELL, CELL))
    full[..., : half + 1] = given
    for plane in (0, half):
        full[..., plane] = 0.5 * (given[..., plane] + turned[..., plane])
    for plane in range(half + 1, CELL):
        full[..., plane] = turned[..., CELL - plane]
    full[:, 3:] *= 0.5
    return full[:, :, : half + 1].reshape(6, 6, half + 1, PLANE)


def cell_tables():
    green = effective_green()
    coefs = np.zeros((9, 24, PLANE))
    for a in range(6):
        for b in range(a, 6):
            coefs[:, packed[(a, b)]] = green[a, b]
    wide = green.transpose(2, 1, 0, 3).reshape(9, 6, 6 * PLANE)
    upper = wide.astype(bf16).astype(np.float64)
    first = np.zeros((9, 32, 6 * PLANE))
    first[:, 0:6] = upper
    first[:, 6:12] = upper
    first[:, 12:18] = wide - upper
    place = np.arange(PLANE)
    phase = (place // CELL)[:, None] * (place // CELL)[None, :] + (place % CELL)[:, None] * (
        place % CELL
    )[None, :]
    angle = (phase % CELL) * (2.0 * math.pi / CELL)
    cos, sin = np.cos(angle), np.sin(angle)
    forward = np.block([[cos, sin], [-sin, cos]])
    inverse = np.block([[cos, -sin], [sin, cos]]) * (2.0 / VOX)
    return coefs, first, forward, inverse, cos + sin, (cos + sin) / VOX


def parts3(value):
    first = value.astype(bf16)
    rest = value - first.astype(f32)
    second = rest.astype(bf16)
    third = (rest - second.astype(f32)).astype(bf16)
    return jnp.concatenate([first, second, third], axis=0)


def total3(value):
    rows = value.shape[0] // 3
    return value[:rows] + value[rows : 2 * rows] + value[2 * rows :]


def forward_x(v):
    s = [v[x] + v[x + 8] for x in range(8)]
    d = [v[x] - v[x + 8] for x in range(8)]
    a = [s[x] + s[x + 4] for x in range(4)]
    b = [s[x] - s[x + 4] for x in range(4)]
    a02, a13 = a[0] + a[2], a[1] + a[3]
    bm, bp = C2 * (b[1] - b[3]), C2 * (b[1] + b[3])
    p1, p2, p3 = d[1] - d[7], C2 * (d[2] - d[6]), d[3] - d[5]
    q1, q2, q3 = d[1] + d[7], C2 * (d[2] + d[6]), d[3] + d[5]
    re_sum, re_dif = d[0] + p2, d[0] - p2
    re_a, re_b = C1 * p1 + C3 * p3, C3 * p1 - C1 * p3
    im_sum, im_dif = q2 + d[4], q2 - d[4]
    im_a, im_b = C3 * q1 + C1 * q3, C1 * q1 - C3 * q3
    pairs = [
        (re_sum + re_a, im_a + im_sum),
        (b[0] + bm, bp + b[2]),
        (re_dif + re_b, im_b + im_dif),
        (a[0] - a[2], a[1] - a[3]),
        (re_dif - re_b, im_b - im_dif),
        (b[0] - bm, bp - b[2]),
        (re_sum - re_a, im_a - im_sum),
    ]
    return a02 + a13, a02 - a13, pairs


def inverse_x(x0, x8, pairs):
    r = [None] + [pair[0] for pair in pairs]
    m = [None] + [pair[1] for pair in pairs]
    plus, minus = x0 + x8, x0 - x8
    r26p, r26m = r[2] + r[6], C2 * (r[2] - r[6])
    p4 = plus + r[4]
    even = [p4 + r26p, minus + r26m, plus - r[4], minus - r26m, p4 - r26p]
    r17p, r17m, r35p, r35m = r[1] + r[7], r[1] - r[7], r[3] + r[5], r[3] - r[5]
    odd = [r17p + r35p, C1 * r17m + C3 * r35m, C2 * (r17p - r35p), C3 * r17m - C1 * r35m]
    cosine = [None] * 9
    for x in range(4):
        cosine[x] = even[x] + odd[x]
        cosine[8 - x] = even[x] - odd[x]
    cosine[4] = even[4]
    m26p = C2 * (m[2] + m[6])
    s_even = [None, m26p + m[4], m[2] - m[6], m26p - m[4]]
    m17p, m17m, m35p, m35m = m[1] + m[7], m[1] - m[7], m[3] + m[5], m[3] - m[5]
    s_odd = [None, C3 * m17p + C1 * m35p, C2 * (m17m + m35m), C1 * m17p - C3 * m35p]
    sine = [None] * 8
    for x in range(1, 4):
        sine[x] = s_odd[x] + s_even[x]
        sine[8 - x] = s_odd[x] - s_even[x]
    sine[4] = m17m - m35m
    out = [None] * 16
    out[0], out[8] = cosine[0], cosine[8]
    for x in range(1, 8):
        out[x] = cosine[x] + sine[x]
        out[16 - x] = cosine[x] - sine[x]
    return out


def damage_of(e):
    energy = e[0] * e[0] + e[1] * e[1] + e[2] * e[2]
    energy = energy + 2.0 * (e[3] * e[3] + e[4] * e[4] + e[5] * e[5])
    return energy / (energy + kappa_sq)


def unit_law(e, shear):
    volume = lam_hat * (e[0] + e[1] + e[2])
    return [2.0 * mu_hat * e[k] + volume for k in range(3)] + [
        (shear * 2.0 * mu_hat) * e[k] for k in range(3, 6)
    ]


def neighbour(steps, across):
    place = lax.axis_index("dom") * across + lax.axis_index("sub") + steps
    return (place // across, place % across)


def kernel(
    layers,
    slots,
    total,
    across,
    count_ref,
    moved_hbm,
    points_hbm,
    modulus_hbm,
    pick_hbm,
    strain_hbm,
    damage_hbm,
    voxel_hbm,
    forward_hbm,
    first_hbm,
    inverse_hbm,
    real_forward_hbm,
    real_inverse_hbm,
    coef_hbm,
    force_hbm,
    force_ref,
    new_hbm,
    field,
    spec_c,
    spec_r,
    back_c,
    back_r,
    freq,
    green,
    macro,
    stress_s,
    acc,
    new_ref,
    nodes_ref,
    forces,
    sent,
    landed_up,
    landed_down,
    moved_ref,
    points_ref,
    modulus_ref,
    pick_tab,
    strain_tab,
    damage_ref,
    voxel_ref,
    forward_tab,
    first_tab,
    inverse_tab,
    real_forward,
    real_inverse,
    coef_tab,
    force_tab,
    in_sems,
    out_sems,
    send_sems,
    recv_sems,
):
    place = lax.axis_index("dom") * across + lax.axis_index("sub")
    barrier = pltpu.get_barrier_semaphore()
    has_below, has_above = place > 0, place < total - 1

    @pl.when(has_below)
    def _():
        pl.semaphore_signal(barrier, inc=1, device_id=neighbour(-1, across), device_id_type=MESH)

    @pl.when(has_above)
    def _():
        pl.semaphore_signal(barrier, inc=1, device_id=neighbour(1, across), device_id_type=MESH)

    sources = (
        moved_hbm,
        points_hbm,
        modulus_hbm,
        pick_hbm,
        strain_hbm,
        damage_hbm,
        voxel_hbm,
        forward_hbm,
        first_hbm,
        inverse_hbm,
        real_forward_hbm,
        real_inverse_hbm,
        coef_hbm,
        force_hbm,
    )
    targets = (
        moved_ref,
        points_ref,
        modulus_ref,
        pick_tab,
        strain_tab,
        damage_ref,
        voxel_ref,
        forward_tab,
        first_tab,
        inverse_tab,
        real_forward,
        real_inverse,
        coef_tab,
        force_tab,
    )
    loads = [
        pltpu.make_async_copy(source, target, in_sems.at[n])
        for n, (source, target) in enumerate(zip(sources, targets))
    ]
    for load in loads:
        load.start()

    loads[0].wait()
    sent[...] = jnp.zeros_like(sent)
    for i in range(3):
        sent[i : i + 1, 0:NODES] = moved_ref[i, layers - 1 : layers, :]
    upward = pltpu.make_async_remote_copy(
        src_ref=sent,
        dst_ref=landed_up,
        send_sem=send_sems.at[0],
        recv_sem=recv_sems.at[0],
        device_id=neighbour(1, across),
        device_id_type=MESH,
    )

    pl.semaphore_wait(barrier, jnp.minimum(place, 1) + jnp.minimum(total - 1 - place, 1))

    @pl.when(has_above)
    def _():
        upward.start()

    nodes_ref[...] = jnp.zeros_like(nodes_ref)
    for z in range(layers):
        for cz in range(2):
            for i in range(3):
                if z + cz > 0:
                    row = z * 8 + cz * 3 + i
                    nodes_ref[row : row + 1, 0:NODES] = moved_ref[i, z + cz - 1 : z + cz, :]
    for load in loads[1:5]:
        load.wait()

    @pl.when(has_below)
    def _():
        upward.wait_recv()
        nodes_ref[0:3, :] = landed_up[0:3, :]

    elems = layers * EXY * EXY
    chunks = slots // ROWS
    count = count_ref[0]

    spread = total3(jnp.dot(parts3(nodes_ref[...]), pick_tab[...], preferred_element_type=f32))
    plane = EXY * EXY
    corners = jnp.concatenate(
        [
            jnp.concatenate(
                [spread[z * 8 : z * 8 + 8, c * plane : (c + 1) * plane] for z in range(layers)],
                axis=1,
            )
            for c in range(4)
        ],
        axis=0,
    )
    strain = jnp.dot(strain_tab[...], corners, precision=HIGHEST, preferred_element_type=f32)
    modulus = modulus_ref[...]
    law = unit_law([strain[k * 8 : k * 8 + 8] for k in range(6)], 1.0)
    stress = jnp.concatenate([modulus * law[k] for k in range(6)], axis=0)
    stress_s[...] = stress

    square = (slots, slots)
    diagonal = lax.broadcasted_iota(jnp.int32, square, 0) == lax.broadcasted_iota(
        jnp.int32, square, 1
    )
    spread_points = jnp.broadcast_to(points_ref[...].astype(f32), square)
    points = jnp.sum(jnp.where(diagonal, spread_points, 0.0), axis=1, keepdims=True)
    points = points.astype(jnp.int32)
    element = points % elems
    gauss = points // elems
    hot = (lax.broadcasted_iota(jnp.int32, (slots, elems), 1) == element).astype(f32).astype(bf16)
    both = parts3(jnp.concatenate([strain, stress], axis=0))
    picked = lax.dot_general(hot, both, (((1,), (1,)), ((), ())), preferred_element_type=f32)
    picked = picked[:, 0:96] + picked[:, 96:192] + picked[:, 192:288]
    lane96 = lax.broadcasted_iota(jnp.int32, (slots, 96), 1)
    own = [
        jnp.sum(jnp.where(lane96 == k * 8 + gauss, picked, 0.0), axis=1, keepdims=True)
        for k in range(12)
    ]
    mean = [own[k].astype(bf16).astype(f32) for k in range(6)]
    for k in range(6):
        macro[k] = jnp.broadcast_to(mean[k], (slots, HALF))

    mean_law = unit_law(mean, 2.0)
    mean_damage = damage_of(mean)
    lane32 = lax.broadcasted_iota(jnp.int32, (slots, 32), 1)
    upper = jnp.zeros((slots, 32), f32)
    for k in range(6):
        high = mean_law[k].astype(bf16).astype(f32)
        upper = jnp.where((lane32 == k) | (lane32 == 12 + k), high, upper)
        upper = jnp.where(lane32 == 6 + k, mean_law[k] - high, upper)
    mean_parts = upper.astype(bf16)
    for load in loads[5:7]:
        load.wait()
    for r in range(chunks):
        rows = slice(r * ROWS, (r + 1) * ROWS)
        for h in range(2):
            lanes = slice(h * HALF, (h + 1) * HALF)
            scalar = []
            for x in range(CELL):
                cols = slice(x * PLANE + h * HALF, x * PLANE + (h + 1) * HALF)
                old = damage_ref[rows, cols].astype(f32)
                young = voxel_ref[rows, cols].astype(f32)
                scalar.append((1.0 - jnp.maximum(old, mean_damage[rows])) * young - ref_modulus)
            x0, x8, pairs = forward_x(scalar)
            spec_r[0, rows, lanes] = x0.astype(bf16)
            spec_r[1, rows, lanes] = x8.astype(bf16)
            for j in range(7):
                spec_c[j, rows, h * HALF : (h + 1) * HALF] = pairs[j][0].astype(bf16)
                spec_c[j, rows, PLANE + h * HALF : PLANE + (h + 1) * HALF] = pairs[j][1].astype(
                    bf16
                )

    def first_c(j, carry):
        spectrum = jnp.dot(spec_c[j, 0:slots], forward_tab[...], preferred_element_type=f32)
        weight = jnp.dot(mean_parts, first_tab[j + 1], preferred_element_type=f32)
        for k in range(6):
            part = weight[:, k * PLANE : (k + 1) * PLANE]
            rows = slice(k * slots, (k + 1) * slots)
            green[rows, 0:PLANE] = (part * spectrum[:, 0:PLANE]).astype(bf16)
            green[rows, PLANE:] = (part * spectrum[:, PLANE:]).astype(bf16)
        wave = jnp.dot(green[...], inverse_tab[...], preferred_element_type=f32)
        back_c[j] = wave.astype(bf16)
        return carry

    def first_r(j, carry):
        spectrum = jnp.dot(spec_r[j, 0:slots], real_forward[...], preferred_element_type=f32)
        weight = jnp.dot(mean_parts, first_tab[j * 8], preferred_element_type=f32)
        for k in range(6):
            part = weight[:, k * PLANE : (k + 1) * PLANE]
            green[k * slots : (k + 1) * slots, 0:PLANE] = (part * spectrum).astype(bf16)
        wave = jnp.dot(green[:, 0:PLANE], real_inverse[...], preferred_element_type=f32)
        back_r[j] = wave.astype(bf16)
        return carry

    def to_strain(k, carry):
        for r in range(chunks):
            rows = pl.ds(pl.multiple_of(k * slots + r * ROWS, ROWS), ROWS)
            base = macro[k, r * ROWS : (r + 1) * ROWS]
            for h in range(2):
                lanes = slice(h * HALF, (h + 1) * HALF)
                upper_lanes = slice(PLANE + h * HALF, PLANE + (h + 1) * HALF)
                pairs = [(back_c[j, rows, lanes], back_c[j, rows, upper_lanes]) for j in range(7)]
                values = inverse_x(back_r[0, rows, lanes], back_r[1, rows, lanes], pairs)
                for x in range(CELL):
                    field[k * CELL + x, r * ROWS : (r + 1) * ROWS, lanes] = (
                        base - values[x].astype(f32)
                    )
        return carry

    for load in loads[7:]:
        load.wait()
    lax.fori_loop(0, 7, first_c, 0)
    lax.fori_loop(0, 2, first_r, 0)
    lax.fori_loop(0, 6, to_strain, 0)

    def polarize(x, carry):
        cols = pl.ds(pl.multiple_of(x * PLANE, PLANE), PLANE)
        for r in range(chunks):
            rows = slice(r * ROWS, (r + 1) * ROWS)
            e = [field[k * CELL + x, rows] for k in range(6)]
            old = damage_ref[rows, cols].astype(f32)
            young = voxel_ref[rows, cols].astype(f32)
            change = (1.0 - jnp.maximum(old, damage_of(e))) * young - ref_modulus
            for k, unit in enumerate(unit_law(e, 2.0)):
                field[k * CELL + x, rows] = change * unit
        return carry

    def to_spectrum(k, carry):
        for r in range(chunks):
            rows = pl.ds(pl.multiple_of(k * slots + r * ROWS, ROWS), ROWS)
            for h in range(2):
                lanes = slice(h * HALF, (h + 1) * HALF)
                upper_lanes = slice(PLANE + h * HALF, PLANE + (h + 1) * HALF)
                x0, x8, pairs = forward_x(
                    [field[k * CELL + x, r * ROWS : (r + 1) * ROWS, lanes] for x in range(CELL)]
                )
                spec_r[0, rows, lanes] = x0.astype(bf16)
                spec_r[1, rows, lanes] = x8.astype(bf16)
                for j in range(7):
                    spec_c[j, rows, lanes] = pairs[j][0].astype(bf16)
                    spec_c[j, rows, upper_lanes] = pairs[j][1].astype(bf16)
        return carry

    def apply_green(index, planes):
        for h in range(2):
            lanes = slice(h * HALF, (h + 1) * HALF)
            coefs = [
                jnp.broadcast_to(coef_tab[index, c : c + 1, lanes], (ROWS, HALF)).astype(bf16)
                for c in range(21)
            ]
            for part in range(planes):
                where = slice(part * PLANE + h * HALF, part * PLANE + (h + 1) * HALF)
                for r in range(chunks):
                    t = [
                        freq[k * slots + r * ROWS : k * slots + (r + 1) * ROWS, where]
                        for k in range(6)
                    ]
                    for k in range(6):
                        total = coefs[packed[(k, 0)]] * t[0]
                        for b in range(1, 6):
                            total = total + coefs[packed[(k, b)]] * t[b]
                        green[k * slots + r * ROWS : k * slots + (r + 1) * ROWS, where] = total

    def second_c(j, carry):
        spectrum = jnp.dot(spec_c[j], forward_tab[...], preferred_element_type=f32)
        freq[...] = spectrum.astype(bf16)
        apply_green(j + 1, 2)
        wave = jnp.dot(green[...], inverse_tab[...], preferred_element_type=f32)
        back_c[j] = wave.astype(bf16)
        return carry

    def second_r(j, carry):
        spectrum = jnp.dot(spec_r[j], real_forward[...], preferred_element_type=f32)
        freq[:, 0:PLANE] = spectrum.astype(bf16)
        apply_green(j * 8, 1)
        wave = jnp.dot(green[:, 0:PLANE], real_inverse[...], preferred_element_type=f32)
        back_r[j] = wave.astype(bf16)
        return carry

    lax.fori_loop(0, CELL, polarize, 0)
    lax.fori_loop(0, 6, to_spectrum, 0)
    lax.fori_loop(0, 7, second_c, 0)
    lax.fori_loop(0, 2, second_r, 0)
    lax.fori_loop(0, 6, to_strain, 0)

    stores = []
    for r in range(chunks):
        rows = slice(r * ROWS, (r + 1) * ROWS)
        live = lax.broadcasted_iota(jnp.int32, (ROWS, PLANE), 0) + r * ROWS < count

        def finish(x, sums, rows=rows, live=live):
            cols = pl.ds(pl.multiple_of(x * PLANE, PLANE), PLANE)
            e = [field[k * CELL + x, rows] for k in range(6)]
            old = damage_ref[rows, cols].astype(f32)
            young = voxel_ref[rows, cols].astype(f32)
            now = jnp.maximum(old, damage_of(e))
            new_ref[rows, cols] = jnp.where(live, now, old).astype(bf16)
            left = (1.0 - now) * young
            out = []
            for k, unit in enumerate(unit_law(e, 1.0)):
                value = left * unit
                out.append(sums[k] + (value[:, 0:HALF] + value[:, HALF:]))
            return tuple(out)

        sums = lax.fori_loop(0, CELL, finish, (jnp.zeros((ROWS, HALF), f32),) * 6)
        for k in range(6):
            acc[k, rows] = sums[k]
        stores.append(pltpu.make_async_copy(new_ref.at[rows], new_hbm.at[rows], out_sems.at[r]))
        stores[r].start()

    alive = lax.broadcasted_iota(jnp.int32, (slots, 1), 0) < count
    lane128 = lax.broadcasted_iota(jnp.int32, (slots, HALF), 1)
    change = jnp.zeros((slots, HALF), f32)
    for k in range(6):
        cell_mean = jnp.sum(acc[k], axis=1, keepdims=True) * (1.0 / VOX)
        delta = jnp.where(alive, cell_mean.astype(bf16).astype(f32) - own[6 + k], 0.0)
        change = jnp.where(lane128 == k * 8 + gauss, delta, change)
    turned = jnp.transpose(change)[0:48]
    stress = stress_s[...] + total3(jnp.dot(parts3(turned), hot, preferred_element_type=f32))
    contrib = jnp.dot(force_tab[...], stress, precision=HIGHEST, preferred_element_type=f32)
    by_layer = jnp.concatenate(
        [
            jnp.concatenate(
                [contrib[c * 8 : c * 8 + 8, z * plane : (z + 1) * plane] for c in range(4)], axis=1
            )
            for z in range(layers)
        ],
        axis=0,
    )
    forces[...] = total3(
        lax.dot_general(
            parts3(by_layer), pick_tab[...], (((1,), (1,)), ((), ())), preferred_element_type=f32
        )
    )

    downward = pltpu.make_async_remote_copy(
        src_ref=forces.at[0:8],
        dst_ref=landed_down,
        send_sem=send_sems.at[1],
        recv_sem=recv_sems.at[1],
        device_id=neighbour(-1, across),
        device_id_type=MESH,
    )

    @pl.when(has_below)
    def _():
        downward.start()

    force_ref[...] = jnp.zeros_like(force_ref)
    for z in range(layers):
        for i in range(3):
            value = forces[z * 8 + 3 + i : z * 8 + 4 + i, :]
            if z + 1 < layers:
                value = value + forces[z * 8 + 8 + i : z * 8 + 9 + i, :]
            force_ref[i * layers + z : i * layers + z + 1, :] = value
    for store in stores:
        store.wait()

    @pl.when(has_above)
    def _():
        downward.wait_recv()
        for i in range(3):
            row = i * layers + layers - 1
            force_ref[row : row + 1, :] = force_ref[row : row + 1, :] + landed_down[i : i + 1, :]
        upward.wait_send()

    @pl.when(has_below)
    def _():
        downward.wait_send()


def run_kernel(count, moved, modulus, points, damage, voxel, line):
    slots = damage.shape[0]
    layers = moved.shape[1]
    to_strain, to_force, pick = macro_tables()
    coefs, first, forward, inverse, real_forward, real_inverse = cell_tables()
    operands = (
        moved,
        points,
        modulus,
        jnp.asarray(pick, bf16),
        jnp.asarray(to_strain, f32),
        damage,
        voxel,
        jnp.asarray(forward, bf16),
        jnp.asarray(first, bf16),
        jnp.asarray(inverse, bf16),
        jnp.asarray(real_forward, bf16),
        jnp.asarray(real_inverse, bf16),
        jnp.asarray(coefs, f32),
        jnp.asarray(to_force, f32),
    )
    vmem, hbm = pl.BlockSpec(memory_space=pltpu.VMEM), pl.BlockSpec(memory_space=pltpu.HBM)
    rows = 6 * slots

    def body(*refs):
        kernel(layers, slots, *line, *refs)

    return pl.pallas_call(
        body,
        out_shape=(
            jax.ShapeDtypeStruct((layers * 4, NODE_PAD), f32),
            jax.ShapeDtypeStruct(damage.shape, bf16),
        ),
        in_specs=[pl.BlockSpec(memory_space=pltpu.SMEM)] + [hbm] * len(operands),
        out_specs=(vmem, hbm),
        scratch_shapes=[
            pltpu.VMEM((6 * CELL, slots, PLANE), f32),
            pltpu.VMEM((7, rows, 2 * PLANE), bf16),
            pltpu.VMEM((2, rows, PLANE), bf16),
            pltpu.VMEM((7, rows, 2 * PLANE), bf16),
            pltpu.VMEM((2, rows, PLANE), bf16),
            pltpu.VMEM((rows, 2 * PLANE), bf16),
            pltpu.VMEM((rows, 2 * PLANE), bf16),
            pltpu.VMEM((6, slots, HALF), f32),
            pltpu.VMEM((48, layers * EXY * EXY), f32),
            pltpu.VMEM((6, slots, HALF), f32),
            pltpu.VMEM(damage.shape, bf16),
            pltpu.VMEM((layers * 8, NODE_PAD), f32),
            pltpu.VMEM((layers * 8, NODE_PAD), f32),
        ]
        + [pltpu.VMEM((8, NODE_PAD), f32)] * 3
        + [pltpu.VMEM(operand.shape, operand.dtype) for operand in operands]
        + [
            pltpu.SemaphoreType.DMA((len(operands),)),
            pltpu.SemaphoreType.DMA((slots // ROWS,)),
            pltpu.SemaphoreType.DMA((2,)),
            pltpu.SemaphoreType.DMA((2,)),
        ],
        compiler_params=pltpu.CompilerParams(
            vmem_limit_bytes=65500 * 1024, collective_id=0, has_side_effects=True
        ),
        cost_estimate=pl.CostEstimate(flops=10**10, bytes_accessed=8 * 10**6, transcendentals=0),
    )(count, *operands)


def body(displacement, macro_modulus, damaged_count, damaged_points, damage, voxel_modulus):
    layers = displacement.shape[1]
    across = lax.axis_size("sub")
    total = lax.axis_size("dom") * across
    force, new_damage = run_kernel(
        damaged_count,
        displacement,
        macro_modulus,
        damaged_points,
        damage,
        voxel_modulus,
        (total, across),
    )
    return (force[: 3 * layers].reshape(3, layers, NODE_PAD)[:, :, :NODES], new_damage)


def solution(mesh):
    return jax.shard_map(
        body,
        mesh=mesh,
        in_specs=(
            P(None, ("dom", "sub"), None),
            P(None, ("dom", "sub")),
            P(("dom", "sub")),
            P(("dom", "sub"), None),
            P(("dom", "sub"), None),
            P(("dom", "sub"), None),
        ),
        out_specs=(P(None, ("dom", "sub"), None), P(("dom", "sub"), None)),
        check_vma=False,
    )
```

```python
import functools
import math

import jax
import jax.numpy as jnp
import numpy as np
from jax import lax
from jax.experimental import pallas as pl
from jax.experimental.pallas import tpu as pltpu
from jax.sharding import PartitionSpec as P

CELL = 16
PLANE = CELL * CELL
VOX = CELL**3
EXY = 16
NODES = (EXY + 1) ** 2
NODE_PAD = 384
HALF = 128
ROWS = 16

lam_hat = 0.2 / 0.72
mu_hat = 1.0 / 2.4
ref_modulus = 2.0
kappa_sq = 4.0
voigt_pairs = ((0, 0), (1, 1), (2, 2), (1, 2), (0, 2), (0, 1))
packed = {}
for _a in range(6):
    for _b in range(_a, 6):
        packed[(_a, _b)] = packed[(_b, _a)] = len(packed) - sum(
            1 for _p in packed if _p[0] > _p[1]
        )
C1, C2, C3 = (math.cos(math.pi * n / 8) for n in (1, 2, 3))
f32, bf16 = jnp.float32, jnp.bfloat16
MESH = pl.DeviceIdType.MESH
HIGHEST = lax.Precision.HIGHEST


def shape_table():
    gauss_coord = 1.0 / math.sqrt(3.0)
    gradients = np.zeros((8, 8, 3))
    for corner in range(8):
        signs = [2 * (corner >> d & 1) - 1 for d in range(3)]
        for gauss_no in range(8):
            coords = [(2 * (gauss_no >> d & 1) - 1) * gauss_coord for d in range(3)]
            factor = [(1.0 + signs[d] * coords[d]) / 2.0 for d in range(3)]
            for d in range(3):
                value = float(signs[d])
                for other in range(3):
                    if other != d:
                        value *= factor[other]
                gradients[corner, gauss_no, d] = value
    return gradients


def macro_tables():
    table = shape_table()
    to_strain = np.zeros((48, 32))
    to_force = np.zeros((32, 48))
    for corner in range(8):
        base = (corner & 3) * 8 + (corner >> 2) * 3
        for k, (a, b) in enumerate(voigt_pairs):
            for q in range(8):
                to_strain[k * 8 + q, base + a] += 0.5 * table[corner, q, b]
                to_strain[k * 8 + q, base + b] += 0.5 * table[corner, q, a]
                to_force[base + a, k * 8 + q] += 0.125 * table[corner, q, b]
                if a != b:
                    to_force[base + b, k * 8 + q] += 0.125 * table[corner, q, a]
    pick = np.zeros((NODE_PAD, 4 * EXY * EXY))
    for cy in range(2):
        for cx in range(2):
            for y in range(EXY):
                for x in range(EXY):
                    column = (2 * cy + cx) * EXY * EXY + y * EXY + x
                    pick[(y + cy) * (EXY + 1) + x + cx, column] = 1.0
    return to_strain, to_force, pick


def green_matrix(nx, ny, nz):
    n = np.stack(np.broadcast_arrays(nx, ny, nz)).astype(np.float64)
    square = (n * n).sum(0)
    inverse = np.where(square > 0.5, 1.0 / np.maximum(square, 1.0), 0.0)
    lam_ref, mu_ref = ref_modulus * lam_hat, ref_modulus * mu_hat
    coupling = (lam_ref + mu_ref) / (mu_ref * (lam_ref + 2.0 * mu_ref))
    out = np.zeros((6, 6) + square.shape)
    for column, (a, b) in enumerate(voigt_pairs):
        traction = np.zeros_like(n)
        traction[a] += n[b]
        if a != b:
            traction[b] += n[a]
        along = (n * traction).sum(0)
        amplitude = inverse * traction / mu_ref - coupling * along * inverse * inverse * n
        for k, (c, d) in enumerate(voigt_pairs):
            out[k, column] = 0.5 * (n[c] * amplitude[d] + n[d] * amplitude[c])
    return out


def effective_green():
    index = np.arange(CELL)
    signed = np.where(index < CELL // 2, index, index - CELL)
    mirror = (-index) % CELL
    half = CELL // 2
    fx, fy = signed[:, None, None], signed[None, :, None]
    given = green_matrix(fx, fy, np.arange(half + 1)[None, None, :])
    turned = given[:, :, mirror][:, :, :, mirror]
    full = np.zeros((6, 6, CELL, CELL, CELL))
    full[..., : half + 1] = given
    for plane in (0, half):
        full[..., plane] = 0.5 * (given[..., plane] + turned[..., plane])
    for plane in range(half + 1, CELL):
        full[..., plane] = turned[..., CELL - plane]
    full[:, 3:] *= 0.5
    return full[:, :, : half + 1].reshape(6, 6, half + 1, PLANE)


def cell_tables():
    green = effective_green()
    coefs = np.zeros((9, 24, PLANE))
    for a in range(6):
        for b in range(a, 6):
            coefs[:, packed[(a, b)]] = green[a, b]
    wide = green.transpose(2, 1, 0, 3).reshape(9, 6, 6 * PLANE)
    upper = wide.astype(bf16).astype(np.float64)
    first = np.zeros((9, 32, 6 * PLANE))
    first[:, 0:6] = upper
    first[:, 6:12] = upper
    first[:, 12:18] = wide - upper
    place = np.arange(PLANE)
    phase = (place // CELL)[:, None] * (place // CELL)[None, :] + (place % CELL)[:, None] * (
        place % CELL
    )[None, :]
    angle = (phase % CELL) * (2.0 * math.pi / CELL)
    cos, sin = np.cos(angle), np.sin(angle)
    forward = np.block([[cos, sin], [-sin, cos]])
    inverse = np.block([[cos, -sin], [sin, cos]]) * (2.0 / VOX)
    return coefs, first, forward, inverse, cos + sin, (cos + sin) / VOX


def parts3(value):
    first = value.astype(bf16)
    rest = value - first.astype(f32)
    second = rest.astype(bf16)
    third = (rest - second.astype(f32)).astype(bf16)
    return jnp.concatenate([first, second, third], axis=0)


def total3(value):
    rows = value.shape[0] // 3
    return value[:rows] + value[rows : 2 * rows] + value[2 * rows :]


def forward_x(v):
    s = [v[x] + v[x + 8] for x in range(8)]
    d = [v[x] - v[x + 8] for x in range(8)]
    a = [s[x] + s[x + 4] for x in range(4)]
    b = [s[x] - s[x + 4] for x in range(4)]
    a02, a13 = a[0] + a[2], a[1] + a[3]
    bm, bp = C2 * (b[1] - b[3]), C2 * (b[1] + b[3])
    p1, p2, p3 = d[1] - d[7], C2 * (d[2] - d[6]), d[3] - d[5]
    q1, q2, q3 = d[1] + d[7], C2 * (d[2] + d[6]), d[3] + d[5]
    re_sum, re_dif = d[0] + p2, d[0] - p2
    re_a, re_b = C1 * p1 + C3 * p3, C3 * p1 - C1 * p3
    im_sum, im_dif = q2 + d[4], q2 - d[4]
    im_a, im_b = C3 * q1 + C1 * q3, C1 * q1 - C3 * q3
    pairs = [
        (re_sum + re_a, im_a + im_sum),
        (b[0] + bm, bp + b[2]),
        (re_dif + re_b, im_b + im_dif),
        (a[0] - a[2], a[1] - a[3]),
        (re_dif - re_b, im_b - im_dif),
        (b[0] - bm, bp - b[2]),
        (re_sum - re_a, im_a - im_sum),
    ]
    return a02 + a13, a02 - a13, pairs


def inverse_x(x0, x8, pairs):
    r = [None] + [pair[0] for pair in pairs]
    m = [None] + [pair[1] for pair in pairs]
    plus, minus = x0 + x8, x0 - x8
    r26p, r26m = r[2] + r[6], C2 * (r[2] - r[6])
    p4 = plus + r[4]
    even = [p4 + r26p, minus + r26m, plus - r[4], minus - r26m, p4 - r26p]
    r17p, r17m, r35p, r35m = r[1] + r[7], r[1] - r[7], r[3] + r[5], r[3] - r[5]
    odd = [r17p + r35p, C1 * r17m + C3 * r35m, C2 * (r17p - r35p), C3 * r17m - C1 * r35m]
    cosine = [None] * 9
    for x in range(4):
        cosine[x] = even[x] + odd[x]
        cosine[8 - x] = even[x] - odd[x]
    cosine[4] = even[4]
    m26p = C2 * (m[2] + m[6])
    s_even = [None, m26p + m[4], m[2] - m[6], m26p - m[4]]
    m17p, m17m, m35p, m35m = m[1] + m[7], m[1] - m[7], m[3] + m[5], m[3] - m[5]
    s_odd = [None, C3 * m17p + C1 * m35p, C2 * (m17m + m35m), C1 * m17p - C3 * m35p]
    sine = [None] * 8
    for x in range(1, 4):
        sine[x] = s_odd[x] + s_even[x]
        sine[8 - x] = s_odd[x] - s_even[x]
    sine[4] = m17m - m35m
    out = [None] * 16
    out[0], out[8] = cosine[0], cosine[8]
    for x in range(1, 8):
        out[x] = cosine[x] + sine[x]
        out[16 - x] = cosine[x] - sine[x]
    return out


def damage_of(e):
    energy = e[0] * e[0] + e[1] * e[1] + e[2] * e[2]
    energy = energy + 2.0 * (e[3] * e[3] + e[4] * e[4] + e[5] * e[5])
    return energy / (energy + kappa_sq)


def unit_law(e, shear):
    volume = lam_hat * (e[0] + e[1] + e[2])
    return [2.0 * mu_hat * e[k] + volume for k in range(3)] + [
        (shear * 2.0 * mu_hat) * e[k] for k in range(3, 6)
    ]


def neighbour(steps, across):
    place = lax.axis_index("dom") * across + lax.axis_index("sub") + steps
    return (place // across, place % across)


def kernel(
    layers,
    slots,
    total,
    across,
    count_ref,
    moved_hbm,
    points_hbm,
    modulus_hbm,
    pick_hbm,
    strain_hbm,
    damage_hbm,
    voxel_hbm,
    forward_hbm,
    first_hbm,
    inverse_hbm,
    real_forward_hbm,
    real_inverse_hbm,
    coef_hbm,
    force_hbm,
    force_ref,
    new_hbm,
    field,
    spec_c,
    spec_r,
    back_c,
    back_r,
    freq,
    green,
    macro,
    stress_s,
    acc,
    new_ref,
    nodes_ref,
    forces,
    sent,
    landed_up,
    landed_down,
    moved_ref,
    points_ref,
    modulus_ref,
    pick_tab,
    strain_tab,
    damage_ref,
    voxel_ref,
    forward_tab,
    first_tab,
    inverse_tab,
    real_forward,
    real_inverse,
    coef_tab,
    force_tab,
    in_sems,
    out_sems,
    send_sems,
    recv_sems,
):
    place = lax.axis_index("dom") * across + lax.axis_index("sub")
    barrier = pltpu.get_barrier_semaphore()
    has_below, has_above = place > 0, place < total - 1

    @pl.when(has_below)
    def _():
        pl.semaphore_signal(barrier, inc=1, device_id=neighbour(-1, across), device_id_type=MESH)

    @pl.when(has_above)
    def _():
        pl.semaphore_signal(barrier, inc=1, device_id=neighbour(1, across), device_id_type=MESH)

    sources = (
        moved_hbm,
        points_hbm,
        modulus_hbm,
        pick_hbm,
        strain_hbm,
        damage_hbm,
        voxel_hbm,
        forward_hbm,
        first_hbm,
        inverse_hbm,
        real_forward_hbm,
        real_inverse_hbm,
        coef_hbm,
        force_hbm,
    )
    targets = (
        moved_ref,
        points_ref,
        modulus_ref,
        pick_tab,
        strain_tab,
        damage_ref,
        voxel_ref,
        forward_tab,
        first_tab,
        inverse_tab,
        real_forward,
        real_inverse,
        coef_tab,
        force_tab,
    )
    loads = [
        pltpu.make_async_copy(source, target, in_sems.at[n])
        for n, (source, target) in enumerate(zip(sources, targets))
    ]
    for load in loads:
        load.start()

    loads[0].wait()
    sent[...] = jnp.zeros_like(sent)
    for i in range(3):
        sent[i : i + 1, 0:NODES] = moved_ref[i, layers - 1 : layers, :]
    upward = pltpu.make_async_remote_copy(
        src_ref=sent,
        dst_ref=landed_up,
        send_sem=send_sems.at[0],
        recv_sem=recv_sems.at[0],
        device_id=neighbour(1, across),
        device_id_type=MESH,
    )

    pl.semaphore_wait(barrier, jnp.minimum(place, 1) + jnp.minimum(total - 1 - place, 1))

    @pl.when(has_above)
    def _():
        upward.start()

    nodes_ref[...] = jnp.zeros_like(nodes_ref)
    for z in range(layers):
        for cz in range(2):
            for i in range(3):
                if z + cz > 0:
                    row = z * 8 + cz * 3 + i
                    nodes_ref[row : row + 1, 0:NODES] = moved_ref[i, z + cz - 1 : z + cz, :]
    for load in loads[1:5]:
        load.wait()

    @pl.when(has_below)
    def _():
        upward.wait_recv()
        nodes_ref[0:3, :] = landed_up[0:3, :]

    elems = layers * EXY * EXY
    chunks = slots // ROWS
    count = count_ref[0]

    spread = total3(jnp.dot(parts3(nodes_ref[...]), pick_tab[...], preferred_element_type=f32))
    plane = EXY * EXY
    corners = jnp.concatenate(
        [
            jnp.concatenate(
                [spread[z * 8 : z * 8 + 8, c * plane : (c + 1) * plane] for z in range(layers)],
                axis=1,
            )
            for c in range(4)
        ],
        axis=0,
    )
    strain = jnp.dot(strain_tab[...], corners, precision=HIGHEST, preferred_element_type=f32)
    modulus = modulus_ref[...]
    law = unit_law([strain[k * 8 : k * 8 + 8] for k in range(6)], 1.0)
    stress = jnp.concatenate([modulus * law[k] for k in range(6)], axis=0)
    stress_s[...] = stress

    square = (slots, slots)
    diagonal = lax.broadcasted_iota(jnp.int32, square, 0) == lax.broadcasted_iota(
        jnp.int32, square, 1
    )
    spread_points = jnp.broadcast_to(points_ref[...].astype(f32), square)
    points = jnp.sum(jnp.where(diagonal, spread_points, 0.0), axis=1, keepdims=True)
    points = points.astype(jnp.int32)
    element = points % elems
    gauss = points // elems
    hot = (lax.broadcasted_iota(jnp.int32, (slots, elems), 1) == element).astype(f32).astype(bf16)
    both = parts3(jnp.concatenate([strain, stress], axis=0))
    picked = lax.dot_general(hot, both, (((1,), (1,)), ((), ())), preferred_element_type=f32)
    picked = picked[:, 0:96] + picked[:, 96:192] + picked[:, 192:288]
    lane96 = lax.broadcasted_iota(jnp.int32, (slots, 96), 1)
    own = [
        jnp.sum(jnp.where(lane96 == k * 8 + gauss, picked, 0.0), axis=1, keepdims=True)
        for k in range(12)
    ]
    mean = [own[k].astype(bf16).astype(f32) for k in range(6)]
    for k in range(6):
        macro[k] = jnp.broadcast_to(mean[k], (slots, HALF))

    mean_law = unit_law(mean, 2.0)
    mean_damage = damage_of(mean)
    lane32 = lax.broadcasted_iota(jnp.int32, (slots, 32), 1)
    upper = jnp.zeros((slots, 32), f32)
    for k in range(6):
        high = mean_law[k].astype(bf16).astype(f32)
        upper = jnp.where((lane32 == k) | (lane32 == 12 + k), high, upper)
        upper = jnp.where(lane32 == 6 + k, mean_law[k] - high, upper)
    mean_parts = upper.astype(bf16)
    for load in loads[5:7]:
        load.wait()
    for r in range(chunks):
        rows = slice(r * ROWS, (r + 1) * ROWS)
        for h in range(2):
            lanes = slice(h * HALF, (h + 1) * HALF)
            scalar = []
            for x in range(CELL):
                cols = slice(x * PLANE + h * HALF, x * PLANE + (h + 1) * HALF)
                old = damage_ref[rows, cols].astype(f32)
                young = voxel_ref[rows, cols].astype(f32)
                scalar.append((1.0 - jnp.maximum(old, mean_damage[rows])) * young - ref_modulus)
            x0, x8, pairs = forward_x(scalar)
            spec_r[0, rows, lanes] = x0.astype(bf16)
            spec_r[1, rows, lanes] = x8.astype(bf16)
            for j in range(7):
                spec_c[j, rows, h * HALF : (h + 1) * HALF] = pairs[j][0].astype(bf16)
                spec_c[j, rows, PLANE + h * HALF : PLANE + (h + 1) * HALF] = pairs[j][1].astype(
                    bf16
                )

    waves = [(spec_c, back_c, j, j + 1, 2) for j in range(7)]
    waves += [(spec_r, back_r, j, j * 8, 1) for j in range(2)]

    def forward_yz(wave, rows):
        spec, _, j, _, planes = waves[wave]
        table = forward_tab if planes == 2 else real_forward
        return jnp.dot(spec[j, 0:rows], table[...], preferred_element_type=f32)

    def inverse_yz(wave):
        _, back, j, _, planes = waves[wave]
        table = inverse_tab if planes == 2 else real_inverse
        value = green[wave % 2, :, 0 : planes * PLANE]
        back[j] = jnp.dot(value, table[...], preferred_element_type=f32).astype(bf16)

    def first_green(wave):
        index, planes = waves[wave][3:]
        spectrum = forward_yz(wave, slots)
        weight = jnp.dot(mean_parts, first_tab[index], preferred_element_type=f32)
        for k in range(6):
            part = weight[:, k * PLANE : (k + 1) * PLANE]
            for plane_no in range(planes):
                lanes = slice(plane_no * PLANE, (plane_no + 1) * PLANE)
                green[wave % 2, k * slots : (k + 1) * slots, lanes] = (
                    part * spectrum[:, lanes]
                ).astype(bf16)

    def to_strain(k, carry):
        for r in range(chunks):
            rows = pl.ds(pl.multiple_of(k * slots + r * ROWS, ROWS), ROWS)
            base = macro[k, r * ROWS : (r + 1) * ROWS]
            for h in range(2):
                lanes = slice(h * HALF, (h + 1) * HALF)
                upper_lanes = slice(PLANE + h * HALF, PLANE + (h + 1) * HALF)
                pairs = [(back_c[j, rows, lanes], back_c[j, rows, upper_lanes]) for j in range(7)]
                values = inverse_x(back_r[0, rows, lanes], back_r[1, rows, lanes], pairs)
                for x in range(CELL):
                    field[k * CELL + x, r * ROWS : (r + 1) * ROWS, lanes] = (
                        base - values[x].astype(f32)
                    )
        return carry

    for load in loads[7:]:
        load.wait()
    first_green(0)
    for wave in range(9):
        if wave < 8:
            first_green(wave + 1)
        inverse_yz(wave)
    lax.fori_loop(0, 6, to_strain, 0)

    def polarize(x, carry):
        cols = pl.ds(pl.multiple_of(x * PLANE, PLANE), PLANE)
        for r in range(chunks):
            rows = slice(r * ROWS, (r + 1) * ROWS)
            e = [field[k * CELL + x, rows] for k in range(6)]
            old = damage_ref[rows, cols].astype(f32)
            young = voxel_ref[rows, cols].astype(f32)
            change = (1.0 - jnp.maximum(old, damage_of(e))) * young - ref_modulus
            for k, unit in enumerate(unit_law(e, 2.0)):
                field[k * CELL + x, rows] = change * unit
        return carry

    def to_spectrum(k, carry):
        for r in range(chunks):
            rows = pl.ds(pl.multiple_of(k * slots + r * ROWS, ROWS), ROWS)
            for h in range(2):
                lanes = slice(h * HALF, (h + 1) * HALF)
                upper_lanes = slice(PLANE + h * HALF, PLANE + (h + 1) * HALF)
                x0, x8, pairs = forward_x(
                    [field[k * CELL + x, r * ROWS : (r + 1) * ROWS, lanes] for x in range(CELL)]
                )
                spec_r[0, rows, lanes] = x0.astype(bf16)
                spec_r[1, rows, lanes] = x8.astype(bf16)
                for j in range(7):
                    spec_c[j, rows, lanes] = pairs[j][0].astype(bf16)
                    spec_c[j, rows, upper_lanes] = pairs[j][1].astype(bf16)
        return carry

    def apply_green(wave):
        index, planes = waves[wave][3:]
        half = wave % 2
        for h in range(2):
            lanes = slice(h * HALF, (h + 1) * HALF)
            coefs = [
                jnp.broadcast_to(coef_tab[index, c : c + 1, lanes], (ROWS, HALF)).astype(bf16)
                for c in range(21)
            ]
            for part in range(planes):
                where = slice(part * PLANE + h * HALF, part * PLANE + (h + 1) * HALF)
                for r in range(chunks):
                    t = [
                        freq[half, k * slots + r * ROWS : k * slots + (r + 1) * ROWS, where]
                        for k in range(6)
                    ]
                    for k in range(6):
                        total = coefs[packed[(k, 0)]] * t[0]
                        for b in range(1, 6):
                            total = total + coefs[packed[(k, b)]] * t[b]
                        green[half, k * slots + r * ROWS : k * slots + (r + 1) * ROWS, where] = (
                            total
                        )

    def second_spectrum(wave):
        lanes = waves[wave][4] * PLANE
        freq[wave % 2, :, 0:lanes] = forward_yz(wave, 6 * slots).astype(bf16)

    lax.fori_loop(0, CELL, polarize, 0)
    lax.fori_loop(0, 6, to_spectrum, 0)
    second_spectrum(0)
    for wave in range(9):
        if wave < 8:
            second_spectrum(wave + 1)
        apply_green(wave)
        inverse_yz(wave)
    lax.fori_loop(0, 6, to_strain, 0)

    stores = []
    for r in range(chunks):
        rows = slice(r * ROWS, (r + 1) * ROWS)
        live = lax.broadcasted_iota(jnp.int32, (ROWS, PLANE), 0) + r * ROWS < count

        def finish(x, sums, rows=rows, live=live):
            cols = pl.ds(pl.multiple_of(x * PLANE, PLANE), PLANE)
            e = [field[k * CELL + x, rows] for k in range(6)]
            old = damage_ref[rows, cols].astype(f32)
            young = voxel_ref[rows, cols].astype(f32)
            now = jnp.maximum(old, damage_of(e))
            new_ref[rows, cols] = jnp.where(live, now, old).astype(bf16)
            left = (1.0 - now) * young
            out = []
            for k, unit in enumerate(unit_law(e, 1.0)):
                value = left * unit
                out.append(sums[k] + (value[:, 0:HALF] + value[:, HALF:]))
            return tuple(out)

        sums = lax.fori_loop(0, CELL, finish, (jnp.zeros((ROWS, HALF), f32),) * 6)
        for k in range(6):
            acc[k, rows] = sums[k]
        stores.append(pltpu.make_async_copy(new_ref.at[rows], new_hbm.at[rows], out_sems.at[r]))
        stores[r].start()

    alive = lax.broadcasted_iota(jnp.int32, (slots, 1), 0) < count
    lane128 = lax.broadcasted_iota(jnp.int32, (slots, HALF), 1)
    change = jnp.zeros((slots, HALF), f32)
    for k in range(6):
        cell_mean = jnp.sum(acc[k], axis=1, keepdims=True) * (1.0 / VOX)
        delta = jnp.where(alive, cell_mean.astype(bf16).astype(f32) - own[6 + k], 0.0)
        change = jnp.where(lane128 == k * 8 + gauss, delta, change)
    turned = jnp.transpose(change)[0:48]
    stress = stress_s[...] + total3(jnp.dot(parts3(turned), hot, preferred_element_type=f32))
    contrib = jnp.dot(force_tab[...], stress, precision=HIGHEST, preferred_element_type=f32)
    by_layer = jnp.concatenate(
        [
            jnp.concatenate(
                [contrib[c * 8 : c * 8 + 8, z * plane : (z + 1) * plane] for c in range(4)], axis=1
            )
            for z in range(layers)
        ],
        axis=0,
    )
    forces[...] = total3(
        lax.dot_general(
            parts3(by_layer), pick_tab[...], (((1,), (1,)), ((), ())), preferred_element_type=f32
        )
    )

    downward = pltpu.make_async_remote_copy(
        src_ref=forces.at[0:8],
        dst_ref=landed_down,
        send_sem=send_sems.at[1],
        recv_sem=recv_sems.at[1],
        device_id=neighbour(-1, across),
        device_id_type=MESH,
    )

    @pl.when(has_below)
    def _():
        downward.start()

    force_ref[...] = jnp.zeros_like(force_ref)
    for z in range(layers):
        for i in range(3):
            value = forces[z * 8 + 3 + i : z * 8 + 4 + i, :]
            if z + 1 < layers:
                value = value + forces[z * 8 + 8 + i : z * 8 + 9 + i, :]
            force_ref[i * layers + z : i * layers + z + 1, :] = value
    for store in stores:
        store.wait()

    @pl.when(has_above)
    def _():
        downward.wait_recv()
        for i in range(3):
            row = i * layers + layers - 1
            force_ref[row : row + 1, :] = force_ref[row : row + 1, :] + landed_down[i : i + 1, :]
        upward.wait_send()

    @pl.when(has_below)
    def _():
        downward.wait_send()


def run_kernel(count, moved, modulus, points, damage, voxel, line):
    slots = damage.shape[0]
    layers = moved.shape[1]
    to_strain, to_force, pick = macro_tables()
    coefs, first, forward, inverse, real_forward, real_inverse = cell_tables()
    operands = (
        moved,
        points,
        modulus,
        jnp.asarray(pick, bf16),
        jnp.asarray(to_strain, f32),
        damage,
        voxel,
        jnp.asarray(forward, bf16),
        jnp.asarray(first, bf16),
        jnp.asarray(inverse, bf16),
        jnp.asarray(real_forward, bf16),
        jnp.asarray(real_inverse, bf16),
        jnp.asarray(coefs, f32),
        jnp.asarray(to_force, f32),
    )
    vmem, hbm = pl.BlockSpec(memory_space=pltpu.VMEM), pl.BlockSpec(memory_space=pltpu.HBM)
    rows = 6 * slots

    def body(*refs):
        kernel(layers, slots, *line, *refs)

    return pl.pallas_call(
        body,
        out_shape=(
            jax.ShapeDtypeStruct((layers * 4, NODE_PAD), f32),
            jax.ShapeDtypeStruct(damage.shape, bf16),
        ),
        in_specs=[pl.BlockSpec(memory_space=pltpu.SMEM)] + [hbm] * len(operands),
        out_specs=(vmem, hbm),
        scratch_shapes=[
            pltpu.VMEM((6 * CELL, slots, PLANE), f32),
            pltpu.VMEM((7, rows, 2 * PLANE), bf16),
            pltpu.VMEM((2, rows, PLANE), bf16),
            pltpu.VMEM((7, rows, 2 * PLANE), bf16),
            pltpu.VMEM((2, rows, PLANE), bf16),
            pltpu.VMEM((2, rows, 2 * PLANE), bf16),
            pltpu.VMEM((2, rows, 2 * PLANE), bf16),
            pltpu.VMEM((6, slots, HALF), f32),
            pltpu.VMEM((48, layers * EXY * EXY), f32),
            pltpu.VMEM((6, slots, HALF), f32),
            pltpu.VMEM(damage.shape, bf16),
            pltpu.VMEM((layers * 8, NODE_PAD), f32),
            pltpu.VMEM((layers * 8, NODE_PAD), f32),
        ]
        + [pltpu.VMEM((8, NODE_PAD), f32)] * 3
        + [pltpu.VMEM(operand.shape, operand.dtype) for operand in operands]
        + [
            pltpu.SemaphoreType.DMA((len(operands),)),
            pltpu.SemaphoreType.DMA((slots // ROWS,)),
            pltpu.SemaphoreType.DMA((2,)),
            pltpu.SemaphoreType.DMA((2,)),
        ],
        compiler_params=pltpu.CompilerParams(
            vmem_limit_bytes=65500 * 1024, collective_id=0, has_side_effects=True
        ),
        cost_estimate=pl.CostEstimate(flops=10**10, bytes_accessed=8 * 10**6, transcendentals=0),
    )(count, *operands)


def body(displacement, macro_modulus, damaged_count, damaged_points, damage, voxel_modulus):
    layers = displacement.shape[1]
    across = lax.axis_size("sub")
    total = lax.axis_size("dom") * across
    force, new_damage = run_kernel(
        damaged_count,
        displacement,
        macro_modulus,
        damaged_points,
        damage,
        voxel_modulus,
        (total, across),
    )
    return (force[: 3 * layers].reshape(3, layers, NODE_PAD)[:, :, :NODES], new_damage)


def solution(mesh):
    return jax.shard_map(
        body,
        mesh=mesh,
        in_specs=(
            P(None, ("dom", "sub"), None),
            P(None, ("dom", "sub")),
            P(("dom", "sub")),
            P(("dom", "sub"), None),
            P(("dom", "sub"), None),
            P(("dom", "sub"), None),
        ),
        out_specs=(P(None, ("dom", "sub"), None), P(("dom", "sub"), None)),
        check_vma=False,
    )
```

```python
import functools
import math

import jax
import jax.numpy as jnp
import numpy as np
from jax import lax
from jax.experimental import pallas as pl
from jax.experimental.pallas import tpu as pltpu
from jax.sharding import PartitionSpec as P

CELL = 16
PLANE = CELL * CELL
VOX = CELL**3
EXY = 16
NODES = (EXY + 1) ** 2
NODE_PAD = 384
HALF = 128
ROWS = 16

lam_hat = 0.2 / 0.72
mu_hat = 1.0 / 2.4
ref_modulus = 2.0
kappa_sq = 4.0
voigt_pairs = ((0, 0), (1, 1), (2, 2), (1, 2), (0, 2), (0, 1))
packed = {}
for _a in range(6):
    for _b in range(_a, 6):
        packed[(_a, _b)] = packed[(_b, _a)] = len(packed) - sum(
            1 for _p in packed if _p[0] > _p[1]
        )
C1, C2, C3 = (math.cos(math.pi * n / 8) for n in (1, 2, 3))
f32, bf16 = jnp.float32, jnp.bfloat16
MESH = pl.DeviceIdType.MESH
HIGHEST = lax.Precision.HIGHEST


def shape_table():
    gauss_coord = 1.0 / math.sqrt(3.0)
    gradients = np.zeros((8, 8, 3))
    for corner in range(8):
        signs = [2 * (corner >> d & 1) - 1 for d in range(3)]
        for gauss_no in range(8):
            coords = [(2 * (gauss_no >> d & 1) - 1) * gauss_coord for d in range(3)]
            factor = [(1.0 + signs[d] * coords[d]) / 2.0 for d in range(3)]
            for d in range(3):
                value = float(signs[d])
                for other in range(3):
                    if other != d:
                        value *= factor[other]
                gradients[corner, gauss_no, d] = value
    return gradients


def macro_tables():
    table = shape_table()
    to_strain = np.zeros((48, 32))
    to_force = np.zeros((32, 48))
    for corner in range(8):
        base = (corner & 3) * 8 + (corner >> 2) * 3
        for k, (a, b) in enumerate(voigt_pairs):
            for q in range(8):
                to_strain[k * 8 + q, base + a] += 0.5 * table[corner, q, b]
                to_strain[k * 8 + q, base + b] += 0.5 * table[corner, q, a]
                to_force[base + a, k * 8 + q] += 0.125 * table[corner, q, b]
                if a != b:
                    to_force[base + b, k * 8 + q] += 0.125 * table[corner, q, a]
    pick = np.zeros((NODE_PAD, 4 * EXY * EXY))
    for cy in range(2):
        for cx in range(2):
            for y in range(EXY):
                for x in range(EXY):
                    column = (2 * cy + cx) * EXY * EXY + y * EXY + x
                    pick[(y + cy) * (EXY + 1) + x + cx, column] = 1.0
    return to_strain, to_force, pick


def green_matrix(nx, ny, nz):
    n = np.stack(np.broadcast_arrays(nx, ny, nz)).astype(np.float64)
    square = (n * n).sum(0)
    inverse = np.where(square > 0.5, 1.0 / np.maximum(square, 1.0), 0.0)
    lam_ref, mu_ref = ref_modulus * lam_hat, ref_modulus * mu_hat
    coupling = (lam_ref + mu_ref) / (mu_ref * (lam_ref + 2.0 * mu_ref))
    out = np.zeros((6, 6) + square.shape)
    for column, (a, b) in enumerate(voigt_pairs):
        traction = np.zeros_like(n)
        traction[a] += n[b]
        if a != b:
            traction[b] += n[a]
        along = (n * traction).sum(0)
        amplitude = inverse * traction / mu_ref - coupling * along * inverse * inverse * n
        for k, (c, d) in enumerate(voigt_pairs):
            out[k, column] = 0.5 * (n[c] * amplitude[d] + n[d] * amplitude[c])
    return out


def effective_green():
    index = np.arange(CELL)
    signed = np.where(index < CELL // 2, index, index - CELL)
    mirror = (-index) % CELL
    half = CELL // 2
    fx, fy = signed[:, None, None], signed[None, :, None]
    given = green_matrix(fx, fy, np.arange(half + 1)[None, None, :])
    turned = given[:, :, mirror][:, :, :, mirror]
    full = np.zeros((6, 6, CELL, CELL, CELL))
    full[..., : half + 1] = given
    for plane in (0, half):
        full[..., plane] = 0.5 * (given[..., plane] + turned[..., plane])
    for plane in range(half + 1, CELL):
        full[..., plane] = turned[..., CELL - plane]
    full[:, 3:] *= 0.5
    return full[:, :, : half + 1].reshape(6, 6, half + 1, PLANE)


def cell_tables():
    green = effective_green()
    coefs = np.zeros((9, 24, PLANE))
    for a in range(6):
        for b in range(a, 6):
            coefs[:, packed[(a, b)]] = green[a, b]
    wide = green.transpose(2, 1, 0, 3).reshape(9, 6, 6 * PLANE)
    upper = wide.astype(bf16).astype(np.float64)
    first = np.zeros((9, 32, 6 * PLANE))
    first[:, 0:6] = upper
    first[:, 6:12] = upper
    first[:, 12:18] = wide - upper
    place = np.arange(PLANE)
    phase = (place // CELL)[:, None] * (place // CELL)[None, :] + (place % CELL)[:, None] * (
        place % CELL
    )[None, :]
    angle = (phase % CELL) * (2.0 * math.pi / CELL)
    cos, sin = np.cos(angle), np.sin(angle)
    forward = np.block([[cos, sin], [-sin, cos]])
    inverse = np.block([[cos, -sin], [sin, cos]]) * (2.0 / VOX)
    return coefs, first, forward, inverse, cos + sin, (cos + sin) / VOX


def parts3(value):
    first = value.astype(bf16)
    rest = value - first.astype(f32)
    second = rest.astype(bf16)
    third = (rest - second.astype(f32)).astype(bf16)
    return jnp.concatenate([first, second, third], axis=0)


def total3(value):
    rows = value.shape[0] // 3
    return value[:rows] + value[rows : 2 * rows] + value[2 * rows :]


def forward_x(v):
    s = [v[x] + v[x + 8] for x in range(8)]
    d = [(v[x] - v[x + 8]).astype(bf16) for x in range(8)]
    a = [s[x] + s[x + 4] for x in range(4)]
    b = [(s[x] - s[x + 4]).astype(bf16) for x in range(4)]
    a02, a13 = a[0] + a[2], a[1] + a[3]
    bm, bp = C2 * (b[1] - b[3]), C2 * (b[1] + b[3])
    p1, p2, p3 = d[1] - d[7], C2 * (d[2] - d[6]), d[3] - d[5]
    q1, q2, q3 = d[1] + d[7], C2 * (d[2] + d[6]), d[3] + d[5]
    re_sum, re_dif = d[0] + p2, d[0] - p2
    re_a, re_b = C1 * p1 + C3 * p3, C3 * p1 - C1 * p3
    im_sum, im_dif = q2 + d[4], q2 - d[4]
    im_a, im_b = C3 * q1 + C1 * q3, C1 * q1 - C3 * q3
    pairs = [
        (re_sum + re_a, im_a + im_sum),
        (b[0] + bm, bp + b[2]),
        (re_dif + re_b, im_b + im_dif),
        (a[0] - a[2], a[1] - a[3]),
        (re_dif - re_b, im_b - im_dif),
        (b[0] - bm, bp - b[2]),
        (re_sum - re_a, im_a - im_sum),
    ]
    return a02 + a13, a02 - a13, pairs


def inverse_x(x0, x8, pairs):
    r = [None] + [pair[0] for pair in pairs]
    m = [None] + [pair[1] for pair in pairs]
    plus, minus = x0 + x8, x0 - x8
    r26p, r26m = r[2] + r[6], C2 * (r[2] - r[6])
    p4 = plus + r[4]
    even = [p4 + r26p, minus + r26m, plus - r[4], minus - r26m, p4 - r26p]
    r17p, r17m, r35p, r35m = r[1] + r[7], r[1] - r[7], r[3] + r[5], r[3] - r[5]
    odd = [r17p + r35p, C1 * r17m + C3 * r35m, C2 * (r17p - r35p), C3 * r17m - C1 * r35m]
    cosine = [None] * 9
    for x in range(4):
        cosine[x] = even[x] + odd[x]
        cosine[8 - x] = even[x] - odd[x]
    cosine[4] = even[4]
    m26p = C2 * (m[2] + m[6])
    s_even = [None, m26p + m[4], m[2] - m[6], m26p - m[4]]
    m17p, m17m, m35p, m35m = m[1] + m[7], m[1] - m[7], m[3] + m[5], m[3] - m[5]
    s_odd = [None, C3 * m17p + C1 * m35p, C2 * (m17m + m35m), C1 * m17p - C3 * m35p]
    sine = [None] * 8
    for x in range(1, 4):
        sine[x] = s_odd[x] + s_even[x]
        sine[8 - x] = s_odd[x] - s_even[x]
    sine[4] = m17m - m35m
    out = [None] * 16
    out[0], out[8] = cosine[0], cosine[8]
    for x in range(1, 8):
        out[x] = cosine[x] + sine[x]
        out[16 - x] = cosine[x] - sine[x]
    return out


def damage_of(e):
    energy = e[0] * e[0] + e[1] * e[1] + e[2] * e[2]
    energy = energy + 2.0 * (e[3] * e[3] + e[4] * e[4] + e[5] * e[5])
    return energy / (energy + kappa_sq)


def unit_law(e, shear):
    volume = lam_hat * (e[0] + e[1] + e[2])
    return [2.0 * mu_hat * e[k] + volume for k in range(3)] + [
        (shear * 2.0 * mu_hat) * e[k] for k in range(3, 6)
    ]


def neighbour(steps, across):
    place = lax.axis_index("dom") * across + lax.axis_index("sub") + steps
    return (place // across, place % across)


def kernel(
    layers,
    slots,
    total,
    across,
    count_ref,
    moved_hbm,
    points_hbm,
    modulus_hbm,
    pick_hbm,
    strain_hbm,
    damage_hbm,
    voxel_hbm,
    forward_hbm,
    first_hbm,
    inverse_hbm,
    real_forward_hbm,
    real_inverse_hbm,
    coef_hbm,
    force_hbm,
    force_ref,
    new_hbm,
    field,
    spec_c,
    spec_r,
    back_c,
    back_r,
    freq,
    green,
    macro,
    stress_s,
    acc,
    new_ref,
    nodes_ref,
    forces,
    sent,
    landed_up,
    landed_down,
    moved_ref,
    points_ref,
    modulus_ref,
    pick_tab,
    strain_tab,
    damage_ref,
    voxel_ref,
    forward_tab,
    first_tab,
    inverse_tab,
    real_forward,
    real_inverse,
    coef_tab,
    force_tab,
    in_sems,
    out_sems,
    send_sems,
    recv_sems,
):
    place = lax.axis_index("dom") * across + lax.axis_index("sub")
    barrier = pltpu.get_barrier_semaphore()
    has_below, has_above = place > 0, place < total - 1

    @pl.when(has_below)
    def _():
        pl.semaphore_signal(barrier, inc=1, device_id=neighbour(-1, across), device_id_type=MESH)

    @pl.when(has_above)
    def _():
        pl.semaphore_signal(barrier, inc=1, device_id=neighbour(1, across), device_id_type=MESH)

    sources = (
        moved_hbm,
        points_hbm,
        modulus_hbm,
        pick_hbm,
        strain_hbm,
        damage_hbm,
        voxel_hbm,
        forward_hbm,
        first_hbm,
        inverse_hbm,
        real_forward_hbm,
        real_inverse_hbm,
        coef_hbm,
        force_hbm,
    )
    targets = (
        moved_ref,
        points_ref,
        modulus_ref,
        pick_tab,
        strain_tab,
        damage_ref,
        voxel_ref,
        forward_tab,
        first_tab,
        inverse_tab,
        real_forward,
        real_inverse,
        coef_tab,
        force_tab,
    )
    loads = [
        pltpu.make_async_copy(source, target, in_sems.at[n])
        for n, (source, target) in enumerate(zip(sources, targets))
    ]
    for load in loads:
        load.start()

    loads[0].wait()
    sent[...] = jnp.zeros_like(sent)
    for i in range(3):
        sent[i : i + 1, 0:NODES] = moved_ref[i, layers - 1 : layers, :]
    upward = pltpu.make_async_remote_copy(
        src_ref=sent,
        dst_ref=landed_up,
        send_sem=send_sems.at[0],
        recv_sem=recv_sems.at[0],
        device_id=neighbour(1, across),
        device_id_type=MESH,
    )

    pl.semaphore_wait(barrier, jnp.minimum(place, 1) + jnp.minimum(total - 1 - place, 1))

    @pl.when(has_above)
    def _():
        upward.start()

    nodes_ref[...] = jnp.zeros_like(nodes_ref)
    for z in range(layers):
        for cz in range(2):
            for i in range(3):
                if z + cz > 0:
                    row = z * 8 + cz * 3 + i
                    nodes_ref[row : row + 1, 0:NODES] = moved_ref[i, z + cz - 1 : z + cz, :]
    for load in loads[1:5]:
        load.wait()

    @pl.when(has_below)
    def _():
        upward.wait_recv()
        nodes_ref[0:3, :] = landed_up[0:3, :]

    elems = layers * EXY * EXY
    chunks = slots // ROWS
    count = count_ref[0]

    spread = total3(jnp.dot(parts3(nodes_ref[...]), pick_tab[...], preferred_element_type=f32))
    plane = EXY * EXY
    corners = jnp.concatenate(
        [
            jnp.concatenate(
                [spread[z * 8 : z * 8 + 8, c * plane : (c + 1) * plane] for z in range(layers)],
                axis=1,
            )
            for c in range(4)
        ],
        axis=0,
    )
    strain = jnp.dot(strain_tab[...], corners, precision=HIGHEST, preferred_element_type=f32)
    modulus = modulus_ref[...]
    law = unit_law([strain[k * 8 : k * 8 + 8] for k in range(6)], 1.0)
    stress = jnp.concatenate([modulus * law[k] for k in range(6)], axis=0)
    stress_s[...] = stress

    square = (slots, slots)
    diagonal = lax.broadcasted_iota(jnp.int32, square, 0) == lax.broadcasted_iota(
        jnp.int32, square, 1
    )
    spread_points = jnp.broadcast_to(points_ref[...].astype(f32), square)
    points = jnp.sum(jnp.where(diagonal, spread_points, 0.0), axis=1, keepdims=True)
    points = points.astype(jnp.int32)
    element = points % elems
    gauss = points // elems
    hot = (lax.broadcasted_iota(jnp.int32, (slots, elems), 1) == element).astype(f32).astype(bf16)
    both = parts3(jnp.concatenate([strain, stress], axis=0))
    picked = lax.dot_general(hot, both, (((1,), (1,)), ((), ())), preferred_element_type=f32)
    picked = picked[:, 0:96] + picked[:, 96:192] + picked[:, 192:288]
    lane96 = lax.broadcasted_iota(jnp.int32, (slots, 96), 1)
    own = [
        jnp.sum(jnp.where(lane96 == k * 8 + gauss, picked, 0.0), axis=1, keepdims=True)
        for k in range(12)
    ]
    mean = [own[k].astype(bf16).astype(f32) for k in range(6)]
    for k in range(6):
        macro[k] = jnp.broadcast_to(mean[k], (slots, HALF))

    mean_law = unit_law(mean, 2.0)
    mean_damage = damage_of(mean)
    lane32 = lax.broadcasted_iota(jnp.int32, (slots, 32), 1)
    upper = jnp.zeros((slots, 32), f32)
    for k in range(6):
        high = mean_law[k].astype(bf16).astype(f32)
        upper = jnp.where((lane32 == k) | (lane32 == 12 + k), high, upper)
        upper = jnp.where(lane32 == 6 + k, mean_law[k] - high, upper)
    mean_parts = upper.astype(bf16)
    for load in loads[5:7]:
        load.wait()
    for r in range(chunks):
        rows = slice(r * ROWS, (r + 1) * ROWS)
        for h in range(2):
            lanes = slice(h * HALF, (h + 1) * HALF)
            scalar = []
            for x in range(CELL):
                cols = slice(x * PLANE + h * HALF, x * PLANE + (h + 1) * HALF)
                old = damage_ref[rows, cols].astype(f32)
                young = voxel_ref[rows, cols].astype(f32)
                scalar.append((1.0 - jnp.maximum(old, mean_damage[rows])) * young - ref_modulus)
            x0, x8, pairs = forward_x(scalar)
            spec_r[0, rows, lanes] = x0.astype(bf16)
            spec_r[1, rows, lanes] = x8.astype(bf16)
            for j in range(7):
                spec_c[j, rows, h * HALF : (h + 1) * HALF] = pairs[j][0].astype(bf16)
                spec_c[j, rows, PLANE + h * HALF : PLANE + (h + 1) * HALF] = pairs[j][1].astype(
                    bf16
                )

    waves = [(spec_c, back_c, j, j + 1, 2) for j in range(7)]
    waves += [(spec_r, back_r, j, j * 8, 1) for j in range(2)]

    def forward_yz(wave, rows):
        spec, _, j, _, planes = waves[wave]
        table = forward_tab if planes == 2 else real_forward
        return jnp.dot(spec[j, 0:rows], table[...], preferred_element_type=f32)

    def inverse_yz(wave):
        _, back, j, _, planes = waves[wave]
        table = inverse_tab if planes == 2 else real_inverse
        value = green[wave % 2, :, 0 : planes * PLANE]
        back[j] = jnp.dot(value, table[...], preferred_element_type=f32).astype(bf16)

    def first_green(wave):
        index, planes = waves[wave][3:]
        spectrum = forward_yz(wave, slots)
        weight = jnp.dot(mean_parts, first_tab[index], preferred_element_type=f32)
        for k in range(6):
            part = weight[:, k * PLANE : (k + 1) * PLANE]
            for plane_no in range(planes):
                lanes = slice(plane_no * PLANE, (plane_no + 1) * PLANE)
                green[wave % 2, k * slots : (k + 1) * slots, lanes] = (
                    part * spectrum[:, lanes]
                ).astype(bf16)

    def to_strain(k, carry):
        for r in range(chunks):
            rows = pl.ds(pl.multiple_of(k * slots + r * ROWS, ROWS), ROWS)
            base = macro[k, r * ROWS : (r + 1) * ROWS]
            for h in range(2):
                lanes = slice(h * HALF, (h + 1) * HALF)
                upper_lanes = slice(PLANE + h * HALF, PLANE + (h + 1) * HALF)
                pairs = [(back_c[j, rows, lanes], back_c[j, rows, upper_lanes]) for j in range(7)]
                values = inverse_x(back_r[0, rows, lanes], back_r[1, rows, lanes], pairs)
                for x in range(CELL):
                    field[k * CELL + x, r * ROWS : (r + 1) * ROWS, lanes] = (
                        base - values[x].astype(f32)
                    )
        return carry

    for load in loads[7:]:
        load.wait()
    first_green(0)
    for wave in range(9):
        if wave < 8:
            first_green(wave + 1)
        inverse_yz(wave)
    lax.fori_loop(0, 6, to_strain, 0)

    def polarize(x, carry):
        cols = pl.ds(pl.multiple_of(x * PLANE, PLANE), PLANE)
        for r in range(chunks):
            rows = slice(r * ROWS, (r + 1) * ROWS)
            e = [field[k * CELL + x, rows] for k in range(6)]
            old = damage_ref[rows, cols].astype(f32)
            young = voxel_ref[rows, cols].astype(f32)
            change = (1.0 - jnp.maximum(old, damage_of(e))) * young - ref_modulus
            for k, unit in enumerate(unit_law(e, 2.0)):
                field[k * CELL + x, rows] = change * unit
        return carry

    def to_spectrum(k, carry):
        for r in range(chunks):
            rows = pl.ds(pl.multiple_of(k * slots + r * ROWS, ROWS), ROWS)
            for h in range(2):
                lanes = slice(h * HALF, (h + 1) * HALF)
                upper_lanes = slice(PLANE + h * HALF, PLANE + (h + 1) * HALF)
                x0, x8, pairs = forward_x(
                    [field[k * CELL + x, r * ROWS : (r + 1) * ROWS, lanes] for x in range(CELL)]
                )
                spec_r[0, rows, lanes] = x0.astype(bf16)
                spec_r[1, rows, lanes] = x8.astype(bf16)
                for j in range(7):
                    spec_c[j, rows, lanes] = pairs[j][0].astype(bf16)
                    spec_c[j, rows, upper_lanes] = pairs[j][1].astype(bf16)
        return carry

    def apply_green(wave):
        index, planes = waves[wave][3:]
        half = wave % 2
        for h in range(2):
            lanes = slice(h * HALF, (h + 1) * HALF)
            coefs = [
                jnp.broadcast_to(coef_tab[index, c : c + 1, lanes], (ROWS, HALF)).astype(bf16)
                for c in range(21)
            ]
            for part in range(planes):
                where = slice(part * PLANE + h * HALF, part * PLANE + (h + 1) * HALF)
                for r in range(chunks):
                    t = [
                        freq[half, k * slots + r * ROWS : k * slots + (r + 1) * ROWS, where]
                        for k in range(6)
                    ]
                    for k in range(6):
                        total = coefs[packed[(k, 0)]] * t[0]
                        for b in range(1, 6):
                            total = total + coefs[packed[(k, b)]] * t[b]
                        green[half, k * slots + r * ROWS : k * slots + (r + 1) * ROWS, where] = (
                            total
                        )

    def second_spectrum(wave):
        lanes = waves[wave][4] * PLANE
        freq[wave % 2, :, 0:lanes] = forward_yz(wave, 6 * slots).astype(bf16)

    lax.fori_loop(0, CELL, polarize, 0, unroll=2)
    lax.fori_loop(0, 6, to_spectrum, 0)
    second_spectrum(0)
    for wave in range(9):
        if wave < 8:
            second_spectrum(wave + 1)
        apply_green(wave)
        inverse_yz(wave)
    lax.fori_loop(0, 6, to_strain, 0)

    stores = []
    for r in range(chunks):
        rows = slice(r * ROWS, (r + 1) * ROWS)
        live = lax.broadcasted_iota(jnp.int32, (ROWS, PLANE), 0) + r * ROWS < count

        def finish(x, sums, rows=rows, live=live):
            cols = pl.ds(pl.multiple_of(x * PLANE, PLANE), PLANE)
            e = [field[k * CELL + x, rows] for k in range(6)]
            old = damage_ref[rows, cols].astype(f32)
            young = voxel_ref[rows, cols].astype(f32)
            now = jnp.maximum(old, damage_of(e))
            new_ref[rows, cols] = jnp.where(live, now, old).astype(bf16)
            left = (1.0 - now) * young
            out = []
            for k, unit in enumerate(unit_law(e, 1.0)):
                value = left * unit
                out.append(sums[k] + (value[:, 0:HALF] + value[:, HALF:]))
            return tuple(out)

        sums = lax.fori_loop(0, CELL, finish, (jnp.zeros((ROWS, HALF), f32),) * 6, unroll=4)
        for k in range(6):
            acc[k, rows] = sums[k]
        stores.append(pltpu.make_async_copy(new_ref.at[rows], new_hbm.at[rows], out_sems.at[r]))
        stores[r].start()

    alive = lax.broadcasted_iota(jnp.int32, (slots, 1), 0) < count
    lane128 = lax.broadcasted_iota(jnp.int32, (slots, HALF), 1)
    change = jnp.zeros((slots, HALF), f32)
    for k in range(6):
        cell_mean = jnp.sum(acc[k], axis=1, keepdims=True) * (1.0 / VOX)
        delta = jnp.where(alive, cell_mean.astype(bf16).astype(f32) - own[6 + k], 0.0)
        change = jnp.where(lane128 == k * 8 + gauss, delta, change)
    turned = jnp.transpose(change)[0:48]
    stress = stress_s[...] + total3(jnp.dot(parts3(turned), hot, preferred_element_type=f32))
    contrib = jnp.dot(force_tab[...], stress, precision=HIGHEST, preferred_element_type=f32)
    by_layer = jnp.concatenate(
        [
            jnp.concatenate(
                [contrib[c * 8 : c * 8 + 8, z * plane : (z + 1) * plane] for c in range(4)], axis=1
            )
            for z in range(layers)
        ],
        axis=0,
    )
    forces[...] = total3(
        lax.dot_general(
            parts3(by_layer), pick_tab[...], (((1,), (1,)), ((), ())), preferred_element_type=f32
        )
    )

    downward = pltpu.make_async_remote_copy(
        src_ref=forces.at[0:8],
        dst_ref=landed_down,
        send_sem=send_sems.at[1],
        recv_sem=recv_sems.at[1],
        device_id=neighbour(-1, across),
        device_id_type=MESH,
    )

    @pl.when(has_below)
    def _():
        downward.start()

    force_ref[...] = jnp.zeros_like(force_ref)
    for z in range(layers):
        for i in range(3):
            value = forces[z * 8 + 3 + i : z * 8 + 4 + i, :]
            if z + 1 < layers:
                value = value + forces[z * 8 + 8 + i : z * 8 + 9 + i, :]
            force_ref[i * layers + z : i * layers + z + 1, :] = value
    for store in stores:
        store.wait()

    @pl.when(has_above)
    def _():
        downward.wait_recv()
        for i in range(3):
            row = i * layers + layers - 1
            force_ref[row : row + 1, :] = force_ref[row : row + 1, :] + landed_down[i : i + 1, :]
        upward.wait_send()

    @pl.when(has_below)
    def _():
        downward.wait_send()


def run_kernel(count, moved, modulus, points, damage, voxel, line):
    slots = damage.shape[0]
    layers = moved.shape[1]
    to_strain, to_force, pick = macro_tables()
    coefs, first, forward, inverse, real_forward, real_inverse = cell_tables()
    operands = (
        moved,
        points,
        modulus,
        jnp.asarray(pick, bf16),
        jnp.asarray(to_strain, f32),
        damage,
        voxel,
        jnp.asarray(forward, bf16),
        jnp.asarray(first, bf16),
        jnp.asarray(inverse, bf16),
        jnp.asarray(real_forward, bf16),
        jnp.asarray(real_inverse, bf16),
        jnp.asarray(coefs, f32),
        jnp.asarray(to_force, f32),
    )
    vmem, hbm = pl.BlockSpec(memory_space=pltpu.VMEM), pl.BlockSpec(memory_space=pltpu.HBM)
    rows = 6 * slots

    def body(*refs):
        kernel(layers, slots, *line, *refs)

    return pl.pallas_call(
        body,
        out_shape=(
            jax.ShapeDtypeStruct((layers * 4, NODE_PAD), f32),
            jax.ShapeDtypeStruct(damage.shape, bf16),
        ),
        in_specs=[pl.BlockSpec(memory_space=pltpu.SMEM)] + [hbm] * len(operands),
        out_specs=(vmem, hbm),
        scratch_shapes=[
            pltpu.VMEM((6 * CELL, slots, PLANE), f32),
            pltpu.VMEM((7, rows, 2 * PLANE), bf16),
            pltpu.VMEM((2, rows, PLANE), bf16),
            pltpu.VMEM((7, rows, 2 * PLANE), bf16),
            pltpu.VMEM((2, rows, PLANE), bf16),
            pltpu.VMEM((2, rows, 2 * PLANE), bf16),
            pltpu.VMEM((2, rows, 2 * PLANE), bf16),
            pltpu.VMEM((6, slots, HALF), f32),
            pltpu.VMEM((48, layers * EXY * EXY), f32),
            pltpu.VMEM((6, slots, HALF), f32),
            pltpu.VMEM(damage.shape, bf16),
            pltpu.VMEM((layers * 8, NODE_PAD), f32),
            pltpu.VMEM((layers * 8, NODE_PAD), f32),
        ]
        + [pltpu.VMEM((8, NODE_PAD), f32)] * 3
        + [pltpu.VMEM(operand.shape, operand.dtype) for operand in operands]
        + [
            pltpu.SemaphoreType.DMA((len(operands),)),
            pltpu.SemaphoreType.DMA((slots // ROWS,)),
            pltpu.SemaphoreType.DMA((2,)),
            pltpu.SemaphoreType.DMA((2,)),
        ],
        compiler_params=pltpu.CompilerParams(
            vmem_limit_bytes=65500 * 1024, collective_id=0, has_side_effects=True
        ),
        cost_estimate=pl.CostEstimate(flops=10**10, bytes_accessed=8 * 10**6, transcendentals=0),
    )(count, *operands)


def body(displacement, macro_modulus, damaged_count, damaged_points, damage, voxel_modulus):
    layers = displacement.shape[1]
    across = lax.axis_size("sub")
    total = lax.axis_size("dom") * across
    force, new_damage = run_kernel(
        damaged_count,
        displacement,
        macro_modulus,
        damaged_points,
        damage,
        voxel_modulus,
        (total, across),
    )
    return (force[: 3 * layers].reshape(3, layers, NODE_PAD)[:, :, :NODES], new_damage)


def solution(mesh):
    return jax.shard_map(
        body,
        mesh=mesh,
        in_specs=(
            P(None, ("dom", "sub"), None),
            P(None, ("dom", "sub")),
            P(("dom", "sub")),
            P(("dom", "sub"), None),
            P(("dom", "sub"), None),
            P(("dom", "sub"), None),
        ),
        out_specs=(P(None, ("dom", "sub"), None), P(("dom", "sub"), None)),
        check_vma=False,
    )
```
